512 devices in a mesh: gx: 16 (over x, z_lo, core), gy: 32 (over z_hi, y).
Axes of the slice: x: 4, y: 8, z: 8 (z_hi: 4, z_lo: 2; z = z_hi * 2 + z_lo), core: 2. Of those that a mesh axis runs over, the one named last changes fastest.
Arguments:
- activator: float32 [56, 1024, 2048], P(None, 'gy', 'gx'), may hold values from 0 to 1
- inhibitor: float32 [56, 1024, 2048], P(None, 'gy', 'gx'), may hold values from 0 to 0.5
- feed_rate: bfloat16 [56, 1024, 2048], P(None, 'gy', 'gx'), may hold values from 0.0019989014 to 0.029907227
- kill_rate: bfloat16 [56, 1024, 2048], P(None, 'gy', 'gx'), may hold values from 0.019897461 to 0.19921875
Outputs:
- activator_out: float32 [56, 1024, 2048], P(None, 'gy', 'gx')
- inhibitor_out: float32 [56, 1024, 2048], P(None, 'gy', 'gx')
The draws below stay inside these ranges and needn't reach their ends.
All inputs are finite; a program needn't handle non-finite values.
Results may differ from the reference program's by a relative error of at most 0.0003.
Values sent between devices are 32-bit elements; how exact they have to be, the bound alone decides.
No kernel may reach another device: no remote copies, remote signals or barrier semaphores. Data moves between devices by JAX's collectives and lax.ppermute only.
A program may use at most 64 MiB of HBM per device.

```python
import math
import jax
import jax.numpy as jnp

CX = 128
CY = 32
NZ = 56
STEPS = 4
NX = 2048
NY = 1024


def stripe_mask(count, block_len, depths):
    place = jnp.arange(count) % block_len
    marked = jnp.zeros((count,), jnp.bool_)
    for depth in depths:
        marked = marked | (place == depth) | (place == block_len - 1 - depth)
    return marked


def draw_activator(key, part):
    key = jax.random.fold_in(key, 11)
    first, second, third, fourth = jax.random.split(key, 4)
    shape = (NZ, NY, NX)
    along_x = stripe_mask(NX, CX, (3,))
    along_y = stripe_mask(NY, CY, (3,))
    marked = along_x[None, None, :] | along_y[None, :, None]
    choose = jax.random.randint(first, shape, 0, 2).astype(jnp.float32)
    upper = jax.random.uniform(second, shape, jnp.float32)
    lower = jax.random.uniform(third, shape, jnp.float32)
    ground = jax.random.uniform(fourth, shape, jnp.float32)
    stripe = choose * (0.85 + 0.15 * upper) + (1.0 - choose) * (0.1 * lower)
    rough = 0.03 * ground
    return jnp.where(marked, stripe, rough)


def draw_inhibitor(key, part):
    key = jax.random.fold_in(key, 23)
    first, second, third, fourth = jax.random.split(key, 4)
    shape = (NZ, NY, NX)
    along_x = stripe_mask(NX, CX, (2, 3))
    along_y = stripe_mask(NY, CY, (3,))
    marked = along_x[None, None, :] | along_y[None, :, None]
    choose = jax.random.randint(first, shape, 0, 2).astype(jnp.float32)
    upper = jax.random.uniform(second, shape, jnp.float32)
    lower = jax.random.uniform(third, shape, jnp.float32)
    ground = jax.random.uniform(fourth, shape, jnp.float32)
    stripe = choose * (0.425 + 0.075 * upper) + (1.0 - choose) * (0.05 * lower)
    rough = 0.015 * ground
    return jnp.where(marked, stripe, rough)


def block_scale(own_key, extent, cuts, least, high):
    loudness, own = 1.0, jax.random.fold_in(own_key, 6)
    for dim, blocks in cuts:
        heights = jnp.exp(jax.random.uniform(jax.random.fold_in(own, dim), (blocks,), jnp.float32, least / len(cuts), high / len(cuts)))
        loudness = loudness * jnp.repeat(heights, extent[dim] // blocks).reshape([-1 if axis == dim else 1 for axis in range(len(extent))])
    return loudness


def setup_inputs(seed: int = 0) -> dict:
    key_of = jax.random.split(jax.random.key(seed), 5)
    activator = draw_activator(jax.random.fold_in(key_of[4], 71), 0)
    inhibitor = draw_inhibitor(jax.random.fold_in(key_of[4], 71), 0)
    feed_rate = jnp.clip(jnp.exp(math.log(0.029907227) - 2.7055024 * jax.random.uniform(key_of[2], (NZ, NY, NX), jnp.float32) ** block_scale(key_of[2], (NZ, NY, NX), ((1, 32), (2, 16)), -0.2, 0.2)), 0.0019989014, 0.029907227).astype(jnp.bfloat16)
    kill_rate = jnp.clip(jnp.exp(math.log(0.19921875) - 2.3038113 * jax.random.uniform(key_of[3], (NZ, NY, NX), jnp.float32) ** block_scale(key_of[3], (NZ, NY, NX), ((1, 32), (2, 16)), -0.2, 0.2)), 0.019897461, 0.19921875).astype(jnp.bfloat16)
    return dict(activator=activator, inhibitor=inhibitor, feed_rate=feed_rate, kill_rate=kill_rate)


def near_sum(field):
    return (jnp.roll(field, 1, 2) + jnp.roll(field, -1, 2)
            + jnp.roll(field, 1, 1) + jnp.roll(field, -1, 1))


def z_laplace(field):
    padded = jnp.pad(field, ((1, 1), (0, 0), (0, 0)), mode="edge")
    return padded[2:] + padded[:-2] - 2.0 * field


def reference(activator, inhibitor, feed_rate, kill_rate):
    conc_u = activator
    conc_v = inhibitor
    feed = feed_rate.astype(jnp.float32)
    kill = kill_rate.astype(jnp.float32)
    for step in range(STEPS):
        react = conc_u * conc_v * conc_v
        new_u = conc_u + 0.24 * (near_sum(conc_u) - 4.0 * conc_u) + 0.01 * z_laplace(conc_u) - react + feed * (1.0 - conc_u)
        new_v = conc_v + 0.12 * (near_sum(conc_v) - 4.0 * conc_v) + 0.005 * z_laplace(conc_v) + react - (feed + kill) * conc_v
        conc_u, conc_v = new_u, new_v
    return conc_u, conc_v
```

```python
import jax
import jax.numpy as jnp
from jax import lax
from jax.experimental import pallas as pl
from jax.experimental.pallas import tpu as pltpu
from jax.sharding import PartitionSpec as P

STEPS = 4
NZ, NY, NX = 56, 32, 128
W = 4
ROWS = NY + 2 * W
TILES = NZ // 8
ZP = NZ + 16
G = 24
VMEM_LIMIT = 48 * 1024 * 1024


def swap_pairs(count, parity):
    pairs = []
    for low in range(parity, count, 2):
        high = (low + 1) % count
        pairs += [(low, high), (high, low)]
    return pairs


def swap(block, axis, parity):
    return lax.ppermute(block, axis, swap_pairs(lax.axis_size(axis), parity))


def lanes():
    return lax.broadcasted_iota(jnp.int32, (8, NX), 1)


def take_lanes(value, index):
    return jnp.take_along_axis(value, index, axis=1, mode="promise_in_bounds")


def row_of(ref, y, tile):
    return ref[pl.ds(y + 8 * NY * tile, 8, stride=NY), :]


def widen(ref, wide):
    def body(i, carry):
        at = pl.ds(pl.multiple_of(i * 128, 128), 128)
        wide[at, :] = ref[at, :].astype(jnp.float32)
        return carry

    lax.fori_loop(0, NZ * NY // 128, body, 0)


def pack_y_kernel(u, v, f, k, out_b, out_a, fw, kw):
    even = lax.rem(lax.axis_index("gy"), 2) == 0
    widen(f, fw)
    widen(k, kw)
    for out, is_low in ((out_b, even), (out_a, jnp.logical_not(even))):
        start = jnp.where(is_low, 0, NY - W)
        start_rate = jnp.where(is_low, 0, NY - W + 1)
        for n, (ref, base, count) in enumerate(
            ((u, start, W), (v, start, W), (fw, start_rate, W - 1), (kw, start_rate, W - 1))
        ):
            first = (0, W, 2 * W, 3 * W - 1)[n]
            for r in range(count):
                for i in range(TILES):
                    out[first + r, 8 * i : 8 * i + 8, :] = row_of(ref, base + r, i)


def pack_y(u, v, f, k):
    shape = jax.ShapeDtypeStruct((4 * W - 2, NZ, NX), jnp.float32)
    return pl.pallas_call(
        pack_y_kernel,
        out_shape=(shape, shape),
        scratch_shapes=[pltpu.VMEM((NZ * NY, NX), jnp.float32)] * 2,
        compiler_params=pltpu.CompilerParams(vmem_limit_bytes=VMEM_LIMIT),
        name="pack_y",
    )(u, v, f, k)


def pack_x_kernel(u, v, f, k, out_b, out_a, fw, kw):
    even = lax.rem(lax.axis_index("gx"), 2) == 0
    widen(f, fw)
    widen(k, kw)
    lane = lanes()
    for n, ref in enumerate((u, v, fw, kw)):

        def body(y, carry):
            place = lax.rem(4 * (y + W), NX)
            mask_r = (lane >= place) & (lane < place + 4)
            place_l = lax.rem(place + 4, NX)
            mask_l = (lane >= place_l) & (lane < place_l + 4)
            new = []
            for i in range(TILES):
                value = pltpu.roll(row_of(ref, y, i), place + 4, 1)
                left, right = carry[i]
                new.append((jnp.where(mask_l, value, left), jnp.where(mask_r, value, right)))
            return tuple(new)

        zero = jnp.zeros((8, NX), jnp.float32)
        packed = lax.fori_loop(0, NY, body, ((zero, zero),) * TILES)
        for i, (left, right) in enumerate(packed):
            left = pltpu.roll(left, NX - 4, 1)
            out_b[n, 8 * i : 8 * i + 8, :] = jnp.where(even, left, right)
            out_a[n, 8 * i : 8 * i + 8, :] = jnp.where(even, right, left)


def pack_x(u, v, f, k):
    shape = jax.ShapeDtypeStruct((4, NZ, NX), jnp.float32)
    return pl.pallas_call(
        pack_x_kernel,
        out_shape=(shape, shape),
        scratch_shapes=[pltpu.VMEM((NZ * NY, NX), jnp.float32)] * 2,
        compiler_params=pltpu.CompilerParams(vmem_limit_bytes=VMEM_LIMIT),
        name="pack_x",
    )(u, v, f, k)


def pack_corner_kernel(x_b, x_a, out_b, out_a):
    even_x = lax.rem(lax.axis_index("gx"), 2) == 0
    even_y = lax.rem(lax.axis_index("gy"), 2) == 0
    lane = lanes()
    for i in range(TILES):
        at = slice(8 * i, 8 * i + 8)
        low = jnp.zeros((8, NX), jnp.float32)
        high = low
        for n in range(4):
            b, a = x_b[n, at, :], x_a[n, at, :]
            for side, value in enumerate((jnp.where(even_x, b, a), jnp.where(even_x, a, b))):
                place = (2 * n + side) * 16
                mask = (lane >= place) & (lane < place + 16)
                low = jnp.where(mask, pltpu.roll(value, (place - 16) % NX, 1), low)
                high = jnp.where(mask, pltpu.roll(value, place, 1), high)
        out_b[at, :] = jnp.where(even_y, low, high)
        out_a[at, :] = jnp.where(even_y, high, low)


def pack_corner(x_b, x_a):
    shape = jax.ShapeDtypeStruct((NZ, NX), jnp.float32)
    return pl.pallas_call(pack_corner_kernel, out_shape=(shape, shape), name="pack_corner")(x_b, x_a)


def step_plane(src_u, src_v, feed, decay, dst_u, dst_v, y):
    for i in range(TILES):
        z = 8 + 8 * i
        u = src_u[y, pl.ds(z, 8), :]
        v = src_v[y, pl.ds(z, 8), :]
        f = feed[y, pl.ds(z, 8), :]
        d = decay[y, pl.ds(z, 8), :]
        near_u = (
            pltpu.roll(u, 1, 1)
            + pltpu.roll(u, NX - 1, 1)
            + (src_u[y - 1, pl.ds(z, 8), :] + src_u[y + 1, pl.ds(z, 8), :])
        )
        near_v = (
            pltpu.roll(v, 1, 1)
            + pltpu.roll(v, NX - 1, 1)
            + (src_v[y - 1, pl.ds(z, 8), :] + src_v[y + 1, pl.ds(z, 8), :])
        )
        along_u = src_u[y, pl.ds(z - 1, 8), :] + src_u[y, pl.ds(z + 1, 8), :]
        along_v = src_v[y, pl.ds(z - 1, 8), :] + src_v[y, pl.ds(z + 1, 8), :]
        react = u * v * v
        new_u = (0.24 * near_u + 0.01 * along_u) + (0.02 * u + f * (1.0 - u)) - react
        new_v = (0.12 * near_v + 0.005 * along_v) + d * v + react
        dst_u[y, pl.ds(z, 8), :] = new_u
        dst_v[y, pl.ds(z, 8), :] = new_v
        if i == 0:
            dst_u[y, pl.ds(7, 1), :] = new_u[:1]
            dst_v[y, pl.ds(7, 1), :] = new_v[:1]
        if i == TILES - 1:
            dst_u[y, pl.ds(8 + NZ, 1), :] = new_u[7:]
            dst_v[y, pl.ds(8 + NZ, 1), :] = new_v[7:]


def put_plane(dst, y, i, value, ends):
    dst[y, pl.ds(8 + 8 * i, 8), :] = value
    if ends and i == 0:
        dst[y, pl.ds(7, 1), :] = value[:1]
    if ends and i == TILES - 1:
        dst[y, pl.ds(8 + NZ, 1), :] = value[7:]


def steps_kernel(
    u, v, f, k, y_b, y_a, x_b, x_a, c_b, c_a, out_u, out_v,
    fw, kw, u0, v0, u1, v1, feed, decay, su0, sv0, su1, sv1, s_feed, s_decay,
):
    even_x = lax.rem(lax.axis_index("gx"), 2) == 0
    even_y = lax.rem(lax.axis_index("gy"), 2) == 0
    widen(f, fw)
    widen(k, kw)
    lane = lanes()

    def own(y, carry):
        for i in range(TILES):
            put_plane(u0, y + W, i, row_of(u, y, i), True)
            put_plane(v0, y + W, i, row_of(v, y, i), True)
            rate = row_of(fw, y, i)
            put_plane(feed, y + W, i, rate, False)
            put_plane(decay, y + W, i, 0.51 - (rate + row_of(kw, y, i)), False)
        return carry

    lax.fori_loop(0, NY, own, 0)

    for src, is_low in ((y_b, even_y), (y_a, jnp.logical_not(even_y))):
        start = jnp.where(is_low, 0, NY + W)
        start_rate = jnp.where(is_low, 1, NY + W)
        for r in range(W):
            for i in range(TILES):
                at = slice(8 * i, 8 * i + 8)
                put_plane(u0, start + r, i, src[r, at, :], True)
                put_plane(v0, start + r, i, src[W + r, at, :], True)
                if r < W - 1:
                    rate = src[2 * W + r, at, :]
                    put_plane(feed, start_rate + r, i, rate, False)
                    put_plane(decay, start_rate + r, i, 0.51 - (rate + src[3 * W - 1 + r, at, :]), False)
    for ref in (feed, decay):
        for r in (0, ROWS - 1):
            for i in range(TILES):
                put_plane(ref, r, i, jnp.zeros((8, NX), jnp.float32), False)

    group = lax.div(lane, G)
    inner = lane - group * G
    own_index = jnp.where(inner < 8, inner + 120, jnp.where(inner >= 16, inner - 16, 0))
    own_lane = (inner < 8) | (inner >= 16)
    halo_d = lax.rem(inner, 4)
    is_right = (inner >= 8) & (inner < 12)
    is_left = (inner >= 12) & (inner < 16)

    def strip(j, carry):
        dense_index = lax.rem(lax.rem(group, 4) * 32 + j * 4 + halo_d, NX)
        is_low = j < W
        corner_group = jnp.where(is_low, 0, 4)
        is_corner = (group == corner_group) & (is_right | is_left)
        side = jnp.where(is_right, 1, 0)
        c_low = jnp.logical_not(jnp.logical_xor(is_low, even_y))
        for i in range(TILES):
            at = slice(8 * i, 8 * i + 8)
            corner = jnp.where(c_low, c_b[at, :], c_a[at, :])
            made = []
            for n, ref in enumerate((u0, v0, feed, decay)):
                value = jnp.zeros((8, NX), jnp.float32)
                for g in range(5):
                    row = ref[8 * g + j, pl.ds(8 + 8 * i, 8), :]
                    value = jnp.where((group == g) & own_lane, take_lanes(row, own_index), value)
                b, a = x_b[n, at, :], x_a[n, at, :]
                halo = jnp.where(
                    is_left,
                    take_lanes(jnp.where(even_x, b, a), dense_index),
                    take_lanes(jnp.where(even_x, a, b), dense_index),
                )
                corner_index = lax.rem((2 * n + side) * 16 + lax.rem(j, 4) * 4 + halo_d, NX)
                halo = jnp.where(is_corner, take_lanes(corner, corner_index), halo)
                made.append((value, halo))
            halo_lane = is_right | is_left
            rate = jnp.where(halo_lane, made[2][1], made[2][0])
            put_plane(su0, j + 1, i, jnp.where(halo_lane, made[0][1], made[0][0]), True)
            put_plane(sv0, j + 1, i, jnp.where(halo_lane, made[1][1], made[1][0]), True)
            put_plane(s_feed, j + 1, i, rate, False)
            put_plane(s_decay, j + 1, i, jnp.where(halo_lane, 0.51 - (rate + made[3][1]), made[3][0]), False)
        return carry

    lax.fori_loop(0, 8, strip, 0)

    main, strips = [(u0, v0), (u1, v1)], [(su0, sv0), (su1, sv1)]
    for step in range(STEPS):
        (mu, mv), (nu, nv) = main[step % 2], main[(step + 1) % 2]

        def main_row(y, carry):
            step_plane(mu, mv, feed, decay, nu, nv, y)
            return carry

        lax.fori_loop(step + 1, ROWS - 1 - step, main_row, 0)

        (tu, tv), (wu, wv) = strips[step % 2], strips[(step + 1) % 2]
        for ref in (tu, tv):
            for i in range(TILES):
                at = pl.ds(8 + 8 * i, 8)
                ref[0, at, :] = pltpu.roll(ref[8, at, :], G, 1)
                ref[9, at, :] = pltpu.roll(ref[1, at, :], NX - G, 1)

        def strip_row(y, carry):
            step_plane(tu, tv, s_feed, s_decay, wu, wv, y)
            return carry

        lax.fori_loop(1, 9, strip_row, 0)

    edge = (lane < 4) | (lane >= 124)

    def finish(y, carry):
        g, j = lax.div(y + W, 8), lax.rem(y + W, 8)
        index = lax.rem(jnp.where(lane < 4, lane + 16, lane + 8) + g * G, NX)
        index = jnp.where(lane < 4, lane + 16 + g * G, jnp.where(lane >= 124, lane - 120 + g * G, 0))
        for i in range(TILES):
            at = pl.ds(8 + 8 * i, 8)
            to = pl.ds(y + 8 * NY * i, 8, stride=NY)
            out_u[to, :] = jnp.where(edge, take_lanes(su0[j + 1, at, :], index), u0[y + W, at, :])
            out_v[to, :] = jnp.where(edge, take_lanes(sv0[j + 1, at, :], index), v0[y + W, at, :])
        return carry

    lax.fori_loop(0, NY, finish, 0)


def steps(*args):
    shape = jax.ShapeDtypeStruct((NZ * NY, NX), jnp.float32)
    wide = pltpu.VMEM((NZ * NY, NX), jnp.float32)
    field = pltpu.VMEM((ROWS, ZP, NX), jnp.float32)
    strip = pltpu.VMEM((10, ZP, NX), jnp.float32)
    return pl.pallas_call(
        steps_kernel,
        out_shape=(shape, shape),
        scratch_shapes=[wide] * 2 + [field] * 6 + [strip] * 6,
        compiler_params=pltpu.CompilerParams(vmem_limit_bytes=VMEM_LIMIT),
        name="steps",
    )(*args)


def shards(activator, inhibitor, feed_rate, kill_rate):
    u, v, f, k = (a.reshape(NZ * NY, NX) for a in (activator, inhibitor, feed_rate, kill_rate))
    send_b, send_a = pack_y(u, v, f, k)
    y_b = swap(send_b, "gy", 1)
    x_send_b, x_send_a = pack_x(u, v, f, k)
    x_b = swap(x_send_b, "gx", 1)
    x_a = swap(x_send_a, "gx", 0)
    y_a = swap(send_a, "gy", 0)
    c_send_b, c_send_a = pack_corner(x_b, x_a)
    c_b = swap(c_send_b, "gy", 1)
    c_a = swap(c_send_a, "gy", 0)
    out_u, out_v = steps(u, v, f, k, y_b, y_a, x_b, x_a, c_b, c_a)
    return out_u.reshape(NZ, NY, NX), out_v.reshape(NZ, NY, NX)


def solution(mesh):
    spec = P(None, "gy", "gx")
    return jax.shard_map(
        shards, mesh=mesh, in_specs=(spec,) * 4, out_specs=(spec,) * 2, check_vma=False
    )
```

```python
import jax
import jax.numpy as jnp
from jax import lax
from jax.experimental import pallas as pl
from jax.experimental.pallas import tpu as pltpu
from jax.sharding import PartitionSpec as P

STEPS = 4
NZ, NY, NX = 56, 32, 128
W = 4
PY = 48
OWN, LOW, HIGH = 8, 4, 40
ROWS = range(LOW, HIGH + 4, 8)
MSG = 4 * W - 2
GROUPS, GZ = 8, NZ // 8
VMEM_LIMIT = 32 * 1024 * 1024
LOAD_VMEM_LIMIT = 57 * 1024 * 1024


def swap_pairs(count, parity):
    pairs = []
    for low in range(parity, count, 2):
        high = (low + 1) % count
        pairs += [(low, high), (high, low)]
    return pairs


def swap(block, axis, parity):
    return lax.ppermute(block, axis, swap_pairs(lax.axis_size(axis), parity))


def is_even(axis):
    return lax.rem(lax.axis_index(axis), 2) == 0


def lanes():
    return lax.broadcasted_iota(jnp.int32, (8, NX), 1)


def turn(value, shift, axis=1):
    shift = shift % value.shape[axis]
    return value if shift == 0 else pltpu.roll(value, shift, axis)


def pallas(kernel, name, limit=VMEM_LIMIT, **kwargs):
    params = pltpu.CompilerParams(vmem_limit_bytes=limit)
    return pl.pallas_call(kernel, name=name, compiler_params=params, **kwargs)


def f32(*shape):
    return jax.ShapeDtypeStruct(shape, jnp.float32)


def load_kernel(u, v, f, k, pu, pv, fs, ks, out_b, out_a, fw, kw, sems):
    own = pl.ds(OWN, NY)
    copies = [
        pltpu.make_async_copy(f, fs, sems.at[0]),
        pltpu.make_async_copy(k, ks, sems.at[1]),
        pltpu.make_async_copy(u, pu.at[:, own, :], sems.at[2]),
        pltpu.make_async_copy(v, pv.at[:, own, :], sems.at[3]),
    ]
    for copy in copies:
        copy.start()
    even = is_even("gy")
    starts = (jnp.where(even, OWN, OWN + 28), jnp.where(even, OWN + 28, OWN))
    rate_starts = (jnp.where(even, 0, 13), jnp.where(even, 13, 0))

    def rates(z, carry):
        for src, wide, at in ((fs, fw, 8), (ks, kw, 11)):
            row = pl.multiple_of(z * NY, NY)
            wide[z, 0:8, :] = src[pl.ds(row, 16), :].astype(jnp.float32)[:8]
            wide[z, 8:16, :] = src[pl.ds(row + 16, 16), :].astype(jnp.float32)[8:]
            for out, start in zip((out_b, out_a), rate_starts):
                out[pl.ds(z * MSG + at, 3), :] = wide[z, pl.ds(start, 3), :]
        return carry

    def fields(z, carry):
        for src, at in ((pu, 0), (pv, 4)):
            for out, start in zip((out_b, out_a), starts):
                out[pl.ds(z * MSG + at, 4), :] = src[z, pl.ds(start, 4), :]
        return carry

    copies[0].wait()
    copies[1].wait()
    lax.fori_loop(0, NZ, rates, 0, unroll=2)
    copies[2].wait()
    copies[3].wait()
    lax.fori_loop(0, NZ, fields, 0, unroll=4)


def load(u, v, f, k):
    edge = pltpu.VMEM((NZ, 16, NX), jnp.float32)
    rates = jax.ShapeDtypeStruct((NZ * NY, NX), jnp.bfloat16)
    padded, message = f32(NZ, PY, NX), f32(NZ * MSG, NX)
    return pallas(
        load_kernel,
        "load",
        LOAD_VMEM_LIMIT,
        out_shape=(padded, padded, rates, rates, message, message),
        in_specs=[pl.BlockSpec(memory_space=pltpu.HBM)] * 4,
        scratch_shapes=[edge, edge, pltpu.SemaphoreType.DMA((4,))],
    )(u, v, f, k)


def pack_x_kernel(u, v, f, k, strips, out_b, out_a):
    even = is_even("gx")
    lane = lanes()
    inner = lax.rem(lane, 16)
    group = lax.div(lane, 16)

    def body(j, carry):
        for n, ref in enumerate((u, v, f, k)):
            right, left = [None] * 4, [None] * 4
            for g in range(GROUPS):
                z = GZ * g + j
                tiles = []
                if n < 2:
                    tiles = [ref[z, pl.ds(OWN + 8 * t, 8), :] for t in range(4)]
                else:
                    for t in range(0, 4, 2):
                        at = pl.multiple_of(z * NY, NY) + 8 * t
                        two = ref[pl.ds(at, 16), :].astype(jnp.float32)
                        tiles += [two[:8], two[8:]]
                for t in range(4):
                    value = turn(tiles[t], 16 * g + 8)
                    right[t] = value if g == 0 else jnp.where(group == g, value, right[t])
            for t in range(4):
                pass
            left_edge = right_edge = None
            for t in range(4):
                strips[n, j, 8 * t : 8 * t + 8, :] = right[t]
                low, high = turn(right[t], 4 * t - 8), turn(right[t], 4 * t - 4)
                here = (inner >= 4 * t) & (inner < 4 * t + 4)
                left_edge = low if t == 0 else jnp.where(here, low, left_edge)
                right_edge = high if t == 0 else jnp.where(here, high, right_edge)
            out_b[n, j] = jnp.where(even, left_edge, right_edge)
            out_a[n, j] = jnp.where(even, right_edge, left_edge)
        return carry

    lax.fori_loop(0, GZ, body, 0)


def pack_x(u, v, f, k):
    edge = f32(4, GZ, 8, NX)
    return pallas(pack_x_kernel, "pack_x", out_shape=(f32(4, GZ, NY, NX), edge, edge))(u, v, f, k)


def pack_corner_kernel(x_b, x_a, out_b, out_a):
    even_x, even_y = is_even("gx"), is_even("gy")
    inner = lax.rem(lanes(), 16)
    top = lax.broadcasted_iota(jnp.int32, (8, NX), 0) < 4

    def body(j, carry):
        rows = []
        for first, base in ((0, 0), (4, 12)):
            sides = []
            for is_right in (True, False):
                value = None
                for n in range(4):
                    b, a = x_b[n, j], x_a[n, j]
                    halo = jnp.where(even_x, a, b) if is_right else jnp.where(even_x, b, a)
                    here = (inner >= 4 * n) & (inner < 4 * n + 4)
                    halo = turn(halo, 4 * n - base)
                    value = halo if n == 0 else jnp.where(here, halo, value)
                sides.append(turn(value, (0 if is_right else 4) - first, 0))
            rows.append(jnp.where(top, sides[0], sides[1]))
        out_b[j] = jnp.where(even_y, rows[0], rows[1])
        out_a[j] = jnp.where(even_y, rows[1], rows[0])
        return carry

    lax.fori_loop(0, GZ, body, 0, unroll=True)


def pack_corner(x_b, x_a):
    return pallas(pack_corner_kernel, "pack_corner", out_shape=(f32(GZ, 8, NX),) * 2)(x_b, x_a)


def x_sums(src_u, src_v, z, rows):
    sums = []
    for ref in (src_u, src_v):
        for row in rows:
            value = ref[z, pl.ds(row, 8), :]
            sums.append(turn(value, 1) + turn(value, -1))
    return tuple(sums)


def step_rows(src_u, src_v, feed, decay, z, below, above, row, x_u, x_v):
    at, down, up = pl.ds(row, 8), pl.ds(row - 1, 8), pl.ds(row + 1, 8)
    u, v, f = src_u[z, at, :], src_v[z, at, :], feed[z, at, :]
    near_u = x_u + (src_u[z, down, :] + src_u[z, up, :])
    near_v = x_v + (src_v[z, down, :] + src_v[z, up, :])
    along_u = src_u[below, at, :] + src_u[above, at, :]
    along_v = src_v[below, at, :] + src_v[above, at, :]
    react = u * (v * v)
    new_u = (0.24 * near_u + 0.01 * along_u) + (f - u * (f - 0.02)) - react
    new_v = (0.12 * near_v + 0.005 * along_v) + decay[z, at, :] * v + react
    return new_u, new_v


def sweep(src, rates, rows, count, place, emit, unroll):
    def body(i, sums):
        z, below, above = place(i)
        ahead = x_sums(*src, place(jnp.minimum(i + 1, count - 1))[0], rows)
        values = [
            step_rows(*src, *rates, z, below, above, row, sums[n], sums[len(rows) + n])
            for n, row in enumerate(rows)
        ]
        emit(z, values)
        return ahead

    lax.fori_loop(0, count, body, x_sums(*src, place(0)[0], rows), unroll=unroll)


def steps_kernel(
    u, v, f, k, y_b, y_a, strips, x_b, x_a, c_b, c_a, out_u, out_v, u0, v0,
    u1, v1, feed, decay, su0, sv0, su1, sv1, s_feed, s_kill, sems,
):
    even_x, even_y = is_even("gx"), is_even("gy")
    lane = lanes()
    inner = lax.rem(lane, 16)
    group = lax.div(lane, 16)
    start = (jnp.where(even_y, LOW, HIGH), jnp.where(even_y, HIGH, LOW))
    rate_start = (jnp.where(even_y, LOW + 1, HIGH), jnp.where(even_y, HIGH, LOW + 1))

    def own(z, carry):
        at = pl.multiple_of(z * NY, NY)
        for t in range(0, 4, 2):
            here, to = pl.ds(at + 8 * t, 16), pl.ds(OWN + 8 * t, 16)
            rate = f[here, :].astype(jnp.float32)
            feed[z, to, :] = rate
            decay[z, to, :] = 0.51 - (rate + k[here, :].astype(jnp.float32))
        for src, to, rate_to in zip((y_b, y_a), start, rate_start):
            at = z * MSG
            u0[z, pl.ds(to, 4), :] = src[pl.ds(at, 4), :]
            v0[z, pl.ds(to, 4), :] = src[pl.ds(at + 4, 4), :]
            rate = src[pl.ds(at + 8, 3), :]
            feed[z, pl.ds(rate_to, 3), :] = rate
            decay[z, pl.ds(rate_to, 3), :] = 0.51 - (rate + src[pl.ds(at + 11, 3), :])
        return carry

    lax.fori_loop(0, NZ, own, 0, unroll=2)

    right_halo = (inner >= 8) & (inner < 12)
    left_halo = (inner >= 4) & (inner < 8)
    right_plane, left_plane = 1, GZ + 3
    s_refs = (su0, sv0, s_feed, s_kill)

    def strip(j, carry):
        for n, ref in enumerate(s_refs):
            b, a = x_b[n, j], x_a[n, j]
            on_right, on_left = jnp.where(even_x, a, b), jnp.where(even_x, b, a)
            for t in range(4):
                to = pl.ds(OWN + 8 * t, 8)
                value = strips[n, j, 8 * t : 8 * t + 8, :]
                ref[j + right_plane, to, :] = jnp.where(right_halo, turn(on_right, 8 - 4 * t), value)
                ref[j + left_plane, to, :] = jnp.where(left_halo, turn(on_left, 4 - 4 * t), value)
        for y, c, to, rate_to in zip((y_b, y_a), (c_b, c_a), start, rate_start):
            fields = rates = None
            for g in range(GROUPS):
                at = (GZ * g + j) * MSG
                one = turn(y[pl.ds(at, 8), :], 16 * g + 8)
                two = turn(y[pl.ds(at + 6, 8), :], 16 * g + 8)
                fields = one if g == 0 else jnp.where(group == g, one, fields)
                rates = two if g == 0 else jnp.where(group == g, two, rates)
            corner = c[j]
            other = turn(corner, 4, 0)
            for plane, mask, lane_at, top in (
                (j + right_plane, right_halo, 8, corner),
                (j + left_plane, left_halo, 4, other),
            ):
                su0[plane, pl.ds(to, 4), :] = jnp.where(mask, turn(top, lane_at), fields)[:4]
                bottom = other if top is corner else corner
                sv0[plane, pl.ds(to, 4), :] = jnp.where(mask, turn(bottom, lane_at - 4), fields)[4:]
                s_feed[plane, pl.ds(rate_to, 3), :] = rates[2:5]
                s_kill[plane, pl.ds(rate_to, 3), :] = rates[5:]
                for n, ref in ((2, s_feed), (3, s_kill)):
                    halo = turn(top, lane_at - 4 * n)[:4]
                    ref[plane, pl.ds(to, 4), :] = jnp.where(mask[:4], halo, ref[plane, pl.ds(to, 4), :])
        for plane in (j + right_plane, j + left_plane):
            for row in ROWS:
                at = pl.ds(row, 8)
                s_kill[plane, at, :] = 0.51 - (s_feed[plane, at, :] + s_kill[plane, at, :])
        return carry

    lax.fori_loop(0, GZ, strip, 0)

    def strip_place(i):
        z = jnp.where(i < GZ, i + right_plane, i - GZ + left_plane)
        return z, z - 1, z + 1

    levels = [(su0, sv0), (su1, sv1)]
    for step in range(STEPS):
        src, dst = levels[step % 2], levels[(step + 1) % 2]
        for ref in src:
            for plane in (right_plane, left_plane):
                for row in ROWS:
                    at = pl.ds(row, 8)
                    first, last = ref[plane, at, :], ref[plane + GZ - 1, at, :]
                    ref[plane - 1, at, :] = jnp.where(group == 0, first, turn(last, 16))
                    ref[plane + GZ, at, :] = jnp.where(group == GROUPS - 1, last, turn(first, -16))

        def strip_emit(z, values, dst=dst):
            for row, (new_u, new_v) in zip(ROWS, values):
                dst[0][z, pl.ds(row, 8), :] = new_u
                dst[1][z, pl.ds(row, 8), :] = new_v

        sweep(src, (s_feed, s_kill), ROWS, 2 * GZ, strip_place, strip_emit, 7)

    for j in range(GZ):
        for old, new in ((su0, su1), (sv0, sv1)):
            for t in range(4):
                at = pl.ds(OWN + 8 * t, 8)
                new[j, at, :] = jnp.where(inner < 8, old[j + right_plane, at, :], old[j + left_plane, at, :])

    def place(i):
        return i, jnp.maximum(i - 1, 0), jnp.minimum(i + 1, NZ - 1)

    edge = (lane < 4) | (lane >= 124)
    levels = [(u0, v0), (u1, v1)]
    for step in range(STEPS):
        src, dst = levels[step % 2], levels[(step + 1) % 2]

        def emit(z, values, dst=dst):
            for row, (new_u, new_v) in zip(ROWS, values):
                dst[0][z, pl.ds(row, 8), :] = new_u
                dst[1][z, pl.ds(row, 8), :] = new_v

        def finish(z, values):
            g = lax.div(z, GZ)
            back = NX - 8 - 16 * g
            for t, (new_u, new_v) in enumerate(values):
                at, to = pl.ds(OWN + 8 * t, 8), pl.ds(pl.multiple_of(z * NY, NY) + 8 * t, 8)
                j = z - g * GZ
                out_u[to, :] = jnp.where(edge, pltpu.roll(su1[j, at, :], back, 1), new_u)
                out_v[to, :] = jnp.where(edge, pltpu.roll(sv1[j, at, :], back, 1), new_v)

        if step < STEPS - 1:
            sweep(src, (feed, decay), ROWS, NZ, place, emit, 8)
        else:
            sweep(src, (feed, decay), range(OWN, OWN + NY, 8), NZ, place, finish, 8)


def steps(*args):
    field = pltpu.VMEM((NZ, PY, NX), jnp.float32)
    strip = pltpu.VMEM((2 * GZ + 4, PY, NX), jnp.float32)
    out, padded = f32(NZ * NY, NX), f32(NZ, PY, NX)
    return pallas(
        steps_kernel,
        "steps",
        out_shape=(out, out, padded, padded),
        input_output_aliases={0: 2, 1: 3},
        scratch_shapes=[field] * 4 + [strip] * 6 + [pltpu.SemaphoreType.DMA((2,))],
    )(*args)[:2]


def shards(activator, inhibitor, feed_rate, kill_rate):
    f, k = feed_rate.reshape(NZ * NY, NX), kill_rate.reshape(NZ * NY, NX)
    u, v, f, k, send_b, send_a = load(activator, inhibitor, f, k)
    y_b = swap(send_b, "gy", 1)
    y_a = swap(send_a, "gy", 0)
    strips, x_send_b, x_send_a = pack_x(u, v, f, k)
    x_b = swap(x_send_b, "gx", 1)
    x_a = swap(x_send_a, "gx", 0)
    c_send_b, c_send_a = pack_corner(x_b, x_a)
    c_b = swap(c_send_b, "gy", 1)
    c_a = swap(c_send_a, "gy", 0)
    out_u, out_v = steps(u, v, f, k, y_b, y_a, strips, x_b, x_a, c_b, c_a)
    return out_u.reshape(NZ, NY, NX), out_v.reshape(NZ, NY, NX)


def solution(mesh):
    spec = P(None, "gy", "gx")
    return jax.shard_map(
        shards, mesh=mesh, in_specs=(spec,) * 4, out_specs=(spec,) * 2, check_vma=False
    )
```

```python
import jax
import jax.numpy as jnp
from jax import lax
from jax.experimental import pallas as pl
from jax.experimental.pallas import tpu as pltpu
from jax.sharding import PartitionSpec as P

STEPS = 4
NZ, NY, NX = 56, 32, 128
W = 4
PY = 48
OWN, LOW, HIGH = 8, 4, 40
MSG = 4 * W - 2
GROUPS, GZ = 8, NZ // 8
CORNER = NZ * MSG
RIGHT, LEFT = 1, GZ + 3
SPLANES = 2 * GZ + 4


def swap_pairs(count, parity):
    pairs = []
    for low in range(parity, count, 2):
        high = (low + 1) % count
        pairs += [(low, high), (high, low)]
    return pairs


def swap(block, axis, parity):
    return lax.ppermute(block, axis, swap_pairs(lax.axis_size(axis), parity))


def is_even(axis):
    return lax.rem(lax.axis_index(axis), 2) == 0


def lanes():
    lane = lax.broadcasted_iota(jnp.int32, (8, NX), 1)
    return lane, lax.rem(lane, 16), lax.div(lane, 16)


def turn(value, shift, axis=1):
    shift = shift % value.shape[axis]
    return value if shift == 0 else pltpu.roll(value, shift, axis)


def vmem(*shape):
    return pltpu.VMEM(shape, jnp.float32)


FIELD = (NZ, PY, NX)
STRIP = (SPLANES, PY, NX)
EDGE = (4, GZ, 8, NX)
MESSAGE = (NZ * MSG + 8 * GZ, NX)


def pallas(kernel, name, megabytes, flops=0, **kwargs):
    return pl.pallas_call(
        kernel,
        name=name,
        compiler_params=pltpu.CompilerParams(vmem_limit_bytes=megabytes * 1024 * 1024),
        cost_estimate=pl.CostEstimate(flops=flops, bytes_accessed=flops // 4, transcendentals=0),
        **kwargs,
    )


def load_kernel(u, v, f, k, pu, pv, feed, decay, su, sv, s_feed, s_decay, out_b, out_a, fs, ks, sems):
    own = pl.ds(OWN, NY)
    copies = [
        pltpu.make_async_copy(f, fs, sems.at[0]),
        pltpu.make_async_copy(k, ks, sems.at[1]),
        pltpu.make_async_copy(u, pu.at[:, own, :], sems.at[2]),
        pltpu.make_async_copy(v, pv.at[:, own, :], sems.at[3]),
    ]
    for copy in copies:
        copy.start()
    even = is_even("gx")
    _, inner, group = lanes()

    def rates(z, carry):
        for t in range(0, 4, 2):
            at, to = pl.ds(pl.multiple_of(z * NY, NY) + 8 * t, 16), pl.ds(OWN + 8 * t, 16)
            rate = fs[at, :].astype(jnp.float32)
            feed[z, to, :] = rate
            decay[z, to, :] = 0.51 - (rate + ks[at, :].astype(jnp.float32))
        return carry

    copies[0].wait()
    copies[1].wait()
    lax.fori_loop(0, NZ, rates, 0, unroll=4)

    for n, src, dst in ((2, feed, s_feed), (3, decay, s_decay), (0, pu, su), (1, pv, sv)):
        if n == 0:
            copies[2].wait()
        if n == 1:
            copies[3].wait()

        def body(j, carry, n=n, src=src, dst=dst):
            left_edge = right_edge = None
            for t in range(4):
                at = pl.ds(OWN + 8 * t, 8)
                both = None
                for g in range(GROUPS):
                    value = turn(src[GZ * g + j, at, :], 16 * g + 8)
                    both = value if g == 0 else jnp.where(group == g, value, both)
                dst[j + RIGHT, at, :] = both
                dst[j + LEFT, at, :] = both
                low, high = turn(both, 4 * t - 8), turn(both, 4 * t - 4)
                here = (inner >= 4 * t) & (inner < 4 * t + 4)
                left_edge = low if t == 0 else jnp.where(here, low, left_edge)
                right_edge = high if t == 0 else jnp.where(here, high, right_edge)
            out_b[n, j] = jnp.where(even, left_edge, right_edge)
            out_a[n, j] = jnp.where(even, right_edge, left_edge)
            return carry

        lax.fori_loop(0, GZ, body, 0, unroll=True)


def load(u, v, f, k):
    f, k = f.reshape(NZ * NY, NX), k.reshape(NZ * NY, NX)
    u, v, f, k = (pltpu.with_memory_space_constraint(a, pltpu.HBM) for a in (u, v, f, k))
    rates = pltpu.VMEM((NZ * NY, NX), jnp.bfloat16)
    return pallas(
        load_kernel,
        "load",
        8,
        out_shape=(vmem(*FIELD),) * 4 + (vmem(*STRIP),) * 4 + (vmem(*EDGE),) * 2,
        in_specs=[pl.BlockSpec(memory_space=pltpu.HBM)] * 4,
        scratch_shapes=[rates, rates, pltpu.SemaphoreType.DMA((4,))],
    )(u, v, f, k)


def pack_y_kernel(u, v, feed, decay, x_b, x_a, out_b, out_a):
    even_x, even_y = is_even("gx"), is_even("gy")
    _, inner, _ = lanes()
    top = lax.broadcasted_iota(jnp.int32, (8, NX), 0) < 4
    starts = (jnp.where(even_y, OWN, OWN + 28), jnp.where(even_y, OWN + 28, OWN))
    rate_starts = (jnp.where(even_y, OWN, OWN + 29), jnp.where(even_y, OWN + 29, OWN))

    def rows(z, carry):
        for out, start, rate_start in zip((out_b, out_a), starts, rate_starts):
            at = z * MSG
            out[pl.ds(at, 4), :] = u[z, pl.ds(start, 4), :]
            out[pl.ds(at + 4, 4), :] = v[z, pl.ds(start, 4), :]
            out[pl.ds(at + 8, 3), :] = feed[z, pl.ds(rate_start, 3), :]
            out[pl.ds(at + 11, 3), :] = decay[z, pl.ds(rate_start, 3), :]
        return carry

    lax.fori_loop(0, NZ, rows, 0, unroll=4)
    for j in range(GZ):
        made = []
        for first, base in ((0, 0), (4, 12)):
            sides = []
            for is_right in (True, False):
                value = None
                for n in range(4):
                    b, a = x_b[n, j], x_a[n, j]
                    halo = jnp.where(even_x, a, b) if is_right else jnp.where(even_x, b, a)
                    here = (inner >= 4 * n) & (inner < 4 * n + 4)
                    halo = turn(halo, 4 * n - base)
                    value = halo if n == 0 else jnp.where(here, halo, value)
                sides.append(turn(value, (0 if is_right else 4) - first, 0))
            made.append(jnp.where(top, sides[0], sides[1]))
        at = pl.ds(CORNER + 8 * j, 8)
        out_b[at, :] = jnp.where(even_y, made[0], made[1])
        out_a[at, :] = jnp.where(even_y, made[1], made[0])


def pack_y(u, v, feed, decay, x_b, x_a):
    return pallas(pack_y_kernel, "pack_y", 8, out_shape=(vmem(*MESSAGE),) * 2)(u, v, feed, decay, x_b, x_a)


def x_sums(src_u, src_v, z, rows):
    sums = []
    for ref in (src_u, src_v):
        for row in rows:
            value = ref[z, pl.ds(row, 8), :]
            sums.append(turn(value, 1) + turn(value, -1))
    return tuple(sums)


def step_rows(src_u, src_v, feed, decay, z, below, above, row, x_u, x_v):
    at, down, up = pl.ds(row, 8), pl.ds(row - 1, 8), pl.ds(row + 1, 8)
    u, v, f = src_u[z, at, :], src_v[z, at, :], feed[z, at, :]
    near_u = x_u + (src_u[z, down, :] + src_u[z, up, :])
    near_v = x_v + (src_v[z, down, :] + src_v[z, up, :])
    along_u = src_u[below, at, :] + src_u[above, at, :]
    along_v = src_v[below, at, :] + src_v[above, at, :]
    react = u * (v * v)
    new_u = (0.24 * near_u + 0.01 * along_u) + (f - u * (f - 0.02)) - react
    new_v = (0.12 * near_v + 0.005 * along_v) + decay[z, at, :] * v + react
    return new_u, new_v


def sweep(src, rates, rows, count, place, emit, unroll):
    def body(i, sums):
        z, below, above = place(i)
        ahead = x_sums(*src, place(jnp.minimum(i + 1, count - 1))[0], rows)
        values = [
            step_rows(*src, *rates, z, below, above, row, sums[n], sums[len(rows) + n])
            for n, row in enumerate(rows)
        ]
        emit(z, values)
        return ahead

    lax.fori_loop(0, count, body, x_sums(*src, place(0)[0], rows), unroll=unroll)


def to_planes(dst, rows):
    def emit(z, values):
        for row, new in zip(rows, values):
            for ref, value in zip(dst, new):
                ref[z, pl.ds(row, 8), :] = value

    return emit


def main_place(i):
    return i, jnp.maximum(i - 1, 0), jnp.minimum(i + 1, NZ - 1)


def strip_place(i):
    z = jnp.where(i < GZ, i + RIGHT, i - GZ + LEFT)
    return z, z - 1, z + 1


def strip_ends(refs, rows, group):
    for ref in refs:
        for plane in (RIGHT, LEFT):
            for row in rows:
                at = pl.ds(row, 8)
                first, last = ref[plane, at, :], ref[plane + GZ - 1, at, :]
                ref[plane - 1, at, :] = jnp.where(group == 0, first, turn(last, 16))
                ref[plane + GZ, at, :] = jnp.where(group == GROUPS - 1, last, turn(first, -16))


def merge_strips(src, dst, rows, inner):
    for old, new in zip(src, dst):
        for j in range(GZ):
            for row in rows:
                at = pl.ds(row, 8)
                new[j, at, :] = jnp.where(inner < 8, old[j + RIGHT, at, :], old[j + LEFT, at, :])


def with_edges(merged, z, row, value, edge):
    g = lax.div(z, GZ)
    piece = merged[z - g * GZ, pl.ds(row, 8), :]
    return jnp.where(edge, pltpu.roll(piece, NX - 8 - 16 * g, 1), value)


INNER_ROWS = (8, 16, 24, 32)
LAST_INNER_ROWS = (12, 20, 28)
BORDER_ROWS = (4, 36)
LAST_BORDER_ROWS = (8, 36)


def interior_kernel(
    u0, v0, feed, decay, x_b, x_a, su0_in, sv0_in, s_feed_in, s_decay_in,
    su0, sv0, s_feed, s_decay, u1, v1, u2, v2, u3, v3, su1, sv1, su2, sv2, su3, sv3, o_u, o_v,
    su4, sv4, mu, mv,
):
    even_x = is_even("gx")
    lane, inner, group = lanes()
    right_halo = (inner >= 8) & (inner < 12)
    left_halo = (inner >= 4) & (inner < 8)

    def halos(j, carry):
        for n, ref in enumerate((su0, sv0, s_feed, s_decay)):
            b, a = x_b[n, j], x_a[n, j]
            on_right, on_left = jnp.where(even_x, a, b), jnp.where(even_x, b, a)
            for t in range(4):
                at = pl.ds(OWN + 8 * t, 8)
                both = ref[j + RIGHT, at, :]
                ref[j + RIGHT, at, :] = jnp.where(right_halo, turn(on_right, 8 - 4 * t), both)
                ref[j + LEFT, at, :] = jnp.where(left_halo, turn(on_left, 4 - 4 * t), both)
        return carry

    lax.fori_loop(0, GZ, halos, 0, unroll=True)

    levels = [(su0, sv0), (su1, sv1), (su2, sv2), (su3, sv3), (su4, sv4)]
    for step in range(STEPS):
        rows = INNER_ROWS if step < STEPS - 1 else LAST_INNER_ROWS
        strip_ends(levels[step], INNER_ROWS, group)
        emit = to_planes(levels[step + 1], rows)
        sweep(levels[step], (s_feed, s_decay), rows, 2 * GZ, strip_place, emit, 7)
    merge_strips((su4, sv4), (mu, mv), LAST_INNER_ROWS, inner)

    levels = [(u0, v0), (u1, v1), (u2, v2), (u3, v3)]
    for step in range(STEPS - 1):
        emit = to_planes(levels[step + 1], INNER_ROWS)
        sweep(levels[step], (feed, decay), INNER_ROWS, NZ, main_place, emit, 8)
    edge = (lane < 4) | (lane >= 124)

    def finish(z, values):
        for row, new in zip(LAST_INNER_ROWS, values):
            for out, merged, value in zip((o_u, o_v), (mu, mv), new):
                out[z, pl.ds(row - OWN, 8), :] = with_edges(merged, z, row, value, edge)

    sweep(levels[-1], (feed, decay), LAST_INNER_ROWS, NZ, main_place, finish, 8)


def interior(u0, v0, feed, decay, x_b, x_a, su0, sv0, s_feed, s_decay):
    out = (vmem(*STRIP),) * 4 + (vmem(*FIELD),) * 6 + (vmem(*STRIP),) * 6 + (vmem(NZ, NY, NX),) * 2
    return pallas(
        interior_kernel,
        "interior",
        4,
        40_000_000,
        out_shape=out,
        input_output_aliases={6: 0, 7: 1, 8: 2, 9: 3},
        scratch_shapes=[vmem(*STRIP)] * 2 + [vmem(GZ, PY, NX)] * 2,
    )(u0, v0, feed, decay, x_b, x_a, su0, sv0, s_feed, s_decay)


N_STATE = 22


def border_kernel(*refs):
    y_b, y_a = refs[:2]
    state = refs[2 + N_STATE : 2 + 2 * N_STATE]
    out_u, out_v, su4, sv4, mu, mv, sems = refs[2 + 2 * N_STATE :]
    (u0, v0, feed, decay, su0, sv0, s_feed, s_decay) = state[:8]
    (u1, v1, u2, v2, u3, v3, su1, sv1, su2, sv2, su3, sv3, o_u, o_v) = state[8:]
    even_y = is_even("gy")
    lane, inner, group = lanes()
    start = (jnp.where(even_y, LOW, HIGH), jnp.where(even_y, HIGH, LOW))
    rate_start = (jnp.where(even_y, LOW + 1, HIGH), jnp.where(even_y, HIGH, LOW + 1))

    def rows(z, carry):
        for src, to, rate_to in zip((y_b, y_a), start, rate_start):
            at = z * MSG
            u0[z, pl.ds(to, 4), :] = src[pl.ds(at, 4), :]
            v0[z, pl.ds(to, 4), :] = src[pl.ds(at + 4, 4), :]
            feed[z, pl.ds(rate_to, 3), :] = src[pl.ds(at + 8, 3), :]
            decay[z, pl.ds(rate_to, 3), :] = src[pl.ds(at + 11, 3), :]
        return carry

    lax.fori_loop(0, NZ, rows, 0, unroll=4)

    right_halo = (inner >= 8) & (inner < 12)
    left_halo = (inner >= 4) & (inner < 8)

    def strip(j, carry):
        for y, to, rate_to in zip((y_b, y_a), start, rate_start):
            fields = rates = None
            for g in range(GROUPS):
                at = (GZ * g + j) * MSG
                one = turn(y[pl.ds(at, 8), :], 16 * g + 8)
                two = turn(y[pl.ds(at + 6, 8), :], 16 * g + 8)
                fields = one if g == 0 else jnp.where(group == g, one, fields)
                rates = two if g == 0 else jnp.where(group == g, two, rates)
            corner = y[pl.ds(CORNER + 8 * j, 8), :]
            other = turn(corner, 4, 0)
            for plane, mask, lane_at, top, bottom in (
                (j + RIGHT, right_halo, 8, corner, other),
                (j + LEFT, left_halo, 4, other, corner),
            ):
                su0[plane, pl.ds(to, 4), :] = jnp.where(mask, turn(top, lane_at), fields)[:4]
                sv0[plane, pl.ds(to, 4), :] = jnp.where(mask, turn(bottom, lane_at - 4), fields)[4:]
                s_feed[plane, pl.ds(rate_to, 3), :] = rates[2:5]
                s_decay[plane, pl.ds(rate_to, 3), :] = rates[5:]
                for n, ref in ((2, s_feed), (3, s_decay)):
                    halo = turn(top, lane_at - 4 * n)[:4]
                    at = pl.ds(to, 4)
                    ref[plane, at, :] = jnp.where(mask[:4], halo, ref[plane, at, :])
        return carry

    lax.fori_loop(0, GZ, strip, 0, unroll=True)

    levels = [(su0, sv0), (su1, sv1), (su2, sv2), (su3, sv3), (su4, sv4)]
    for step in range(STEPS):
        rows_now = BORDER_ROWS if step < STEPS - 1 else LAST_BORDER_ROWS
        strip_ends(levels[step], BORDER_ROWS, group)
        emit = to_planes(levels[step + 1], rows_now)
        sweep(levels[step], (s_feed, s_decay), rows_now, 2 * GZ, strip_place, emit, 14)
    merge_strips((su4, sv4), (mu, mv), LAST_BORDER_ROWS, inner)

    levels = [(u0, v0), (u1, v1), (u2, v2), (u3, v3)]
    for step in range(STEPS - 1):
        emit = to_planes(levels[step + 1], BORDER_ROWS)
        sweep(levels[step], (feed, decay), BORDER_ROWS, NZ, main_place, emit, 14)
    edge = (lane < 4) | (lane >= 124)

    def finish(z, values):
        for row, to, new in zip(LAST_BORDER_ROWS, (0, NY - 4), values):
            for out, merged, value in zip((o_u, o_v), (mu, mv), new):
                out[z, pl.ds(to, 4), :] = with_edges(merged, z, row, value, edge)[:4]

    copies = []
    part = NZ // 4
    for c in range(4):

        def place(i, c=c):
            return main_place(i + c * part)

        sweep(levels[-1], (feed, decay), LAST_BORDER_ROWS, part, place, finish, part)
        for n, (src, dst) in enumerate(((o_u, out_u), (o_v, out_v))):
            at = pl.ds(c * part, part)
            copies.append(pltpu.make_async_copy(src.at[at], dst.at[at], sems.at[2 * c + n]))
            copies[-1].start()
    for copy in copies:
        copy.wait()


def border(y_b, y_a, *state):
    out = tuple(vmem(*a.shape) for a in state) + (jax.ShapeDtypeStruct((NZ, NY, NX), jnp.float32),) * 2
    specs = [pl.BlockSpec(memory_space=pltpu.VMEM)] * N_STATE + [pl.BlockSpec(memory_space=pltpu.HBM)] * 2
    return pallas(
        border_kernel,
        "border",
        4,
        20_000_000,
        out_shape=out,
        out_specs=tuple(specs),
        input_output_aliases={2 + n: n for n in range(N_STATE)},
        scratch_shapes=[vmem(*STRIP)] * 2 + [vmem(GZ, PY, NX)] * 2 + [pltpu.SemaphoreType.DMA((8,))],
    )(y_b, y_a, *state)[N_STATE:]


def shards(activator, inhibitor, feed_rate, kill_rate):
    u0, v0, feed, decay, su0, sv0, s_feed, s_decay, x_send_b, x_send_a = load(
        activator, inhibitor, feed_rate, kill_rate
    )
    x_b = swap(x_send_b, "gx", 1)
    x_a = swap(x_send_a, "gx", 0)
    send_b, send_a = pack_y(u0, v0, feed, decay, x_b, x_a)
    y_b = swap(send_b, "gy", 1)
    y_a = swap(send_a, "gy", 0)
    made = interior(u0, v0, feed, decay, x_b, x_a, su0, sv0, s_feed, s_decay)
    return border(y_b, y_a, u0, v0, feed, decay, *made)


def solution(mesh):
    spec = P(None, "gy", "gx")
    return jax.shard_map(
        shards, mesh=mesh, in_specs=(spec,) * 4, out_specs=(spec,) * 2, check_vma=False
    )
```

```python
import jax
import jax.numpy as jnp
from jax import lax
from jax.experimental import pallas as pl
from jax.experimental.pallas import tpu as pltpu
from jax.sharding import PartitionSpec as P

STEPS = 4
NZ, NY, NX = 56, 32, 128
W = 4
PY = 48
OWN, LOW, HIGH = 8, 4, 40
GROUPS, GZ = 8, NZ // 8
FIELDS, RATES = 2 * W, 2 * (W - 1)
CORNER = NZ * FIELDS
TAIL = CORNER + 8 * GZ
RATE_ROWS = NZ * RATES + 8
RIGHT, LEFT = 1, GZ + 3
SPLANES = 2 * GZ + 4


def swap_pairs(count, parity):
    pairs = []
    for low in range(parity, count, 2):
        high = (low + 1) % count
        pairs += [(low, high), (high, low)]
    return pairs


def swap(block, axis, parity):
    return lax.ppermute(block, axis, swap_pairs(lax.axis_size(axis), parity))


SPAN = 8


def relay_pairs(count):
    pairs = []
    for i in range(count):
        run, place = divmod(i, SPAN)
        runs = count // SPAN
        step = {0: -1, SPAN - 1: 1}.get(place, 0)
        pairs.append((i, (run + step) % runs * SPAN + place))
    return pairs


def second_pairs(count):
    pairs = []
    for i in range(count):
        run, place = divmod(i, SPAN)
        other = (place + 1 if place % 2 else place - 1) % SPAN
        pairs.append((i, run * SPAN + other))
    return pairs


def relay(block, axis):
    count = lax.axis_size(axis)
    return lax.ppermute(block, axis, relay_pairs(count)) if count % SPAN == 0 else block


def after_relay(block, axis):
    count = lax.axis_size(axis)
    return lax.ppermute(block, axis, second_pairs(count) if count % SPAN == 0 else swap_pairs(count, 1))


def is_even(axis):
    return lax.rem(lax.axis_index(axis), 2) == 0


def lanes():
    lane = lax.broadcasted_iota(jnp.int32, (8, NX), 1)
    return lane, lax.rem(lane, 16), lax.div(lane, 16)


def turn(value, shift, axis=1):
    shift = shift % value.shape[axis]
    return value if shift == 0 else pltpu.roll(value, shift, axis)


def vmem(*shape):
    return pltpu.VMEM(shape, jnp.float32)


FIELD = (NZ, PY, NX)
STRIP = (SPLANES, PY, NX)
EDGE = (4, GZ, 8, NX)


def pallas(kernel, name, megabytes, flops=0, **kwargs):
    return pl.pallas_call(
        kernel,
        name=name,
        compiler_params=pltpu.CompilerParams(vmem_limit_bytes=megabytes * 1024 * 1024),
        cost_estimate=pl.CostEstimate(flops=flops, bytes_accessed=flops // 4, transcendentals=0),
        **kwargs,
    )


def load_kernel(u, v, f, k, pu, pv, feed, decay, su, sv, s_feed, s_decay, out_b, out_a, fs, ks, sems):
    own = pl.ds(OWN, NY)
    copies = [
        pltpu.make_async_copy(f, fs, sems.at[0]),
        pltpu.make_async_copy(k, ks, sems.at[1]),
        pltpu.make_async_copy(u, pu.at[:, own, :], sems.at[2]),
        pltpu.make_async_copy(v, pv.at[:, own, :], sems.at[3]),
    ]
    for copy in copies:
        copy.start()
    even = is_even("gx")
    _, inner, group = lanes()

    def rates(z, carry):
        for t in range(0, 4, 2):
            at, to = pl.ds(pl.multiple_of(z * NY, NY) + 8 * t, 16), pl.ds(OWN + 8 * t, 16)
            rate = fs[at, :].astype(jnp.float32)
            feed[z, to, :] = rate
            decay[z, to, :] = 0.51 - (rate + ks[at, :].astype(jnp.float32))
        return carry

    copies[0].wait()
    copies[1].wait()
    lax.fori_loop(0, NZ, rates, 0, unroll=4)

    def pack(arrays):
        def body(j, carry):
            for n, src, dst in arrays:
                left_edge = right_edge = None
                for t in range(4):
                    at = pl.ds(OWN + 8 * t, 8)
                    both = None
                    for g in range(GROUPS):
                        value = turn(src[GZ * g + j, at, :], 16 * g + 8)
                        both = value if g == 0 else jnp.where(group == g, value, both)
                    dst[j + RIGHT, at, :] = both
                    dst[j + LEFT, at, :] = both
                    low, high = turn(both, 4 * t - 8), turn(both, 4 * t - 4)
                    here = (inner >= 4 * t) & (inner < 4 * t + 4)
                    left_edge = low if t == 0 else jnp.where(here, low, left_edge)
                    right_edge = high if t == 0 else jnp.where(here, high, right_edge)
                out_b[n, j] = jnp.where(even, left_edge, right_edge)
                out_a[n, j] = jnp.where(even, right_edge, left_edge)
            return carry

        lax.fori_loop(0, GZ, body, 0, unroll=2)

    pack(((2, feed, s_feed), (3, decay, s_decay)))
    copies[2].wait()
    copies[3].wait()
    pack(((0, pu, su), (1, pv, sv)))


def load(u, v, f, k):
    f, k = f.reshape(NZ * NY, NX), k.reshape(NZ * NY, NX)
    u, v, f, k = (pltpu.with_memory_space_constraint(a, pltpu.HBM) for a in (u, v, f, k))
    rates = pltpu.VMEM((NZ * NY, NX), jnp.bfloat16)
    return pallas(
        load_kernel,
        "load",
        8,
        out_shape=(vmem(*FIELD),) * 4 + (vmem(*STRIP),) * 4 + (vmem(*EDGE),) * 2,
        in_specs=[pl.BlockSpec(memory_space=pltpu.HBM)] * 4,
        scratch_shapes=[rates, rates, pltpu.SemaphoreType.DMA((4,))],
    )(u, v, f, k)


def pack_rates_kernel(feed, decay, out):
    start = jnp.where(is_even("gy"), OWN, OWN + 29)

    def rows(z, carry):
        out[pl.ds(RATES * z, 3), :] = feed[z, pl.ds(start, 3), :]
        out[pl.ds(RATES * z + 3, 3), :] = decay[z, pl.ds(start, 3), :]
        return carry

    lax.fori_loop(0, NZ, rows, 0, unroll=8)
    out[pl.ds(RATES * NZ, 8), :] = jnp.zeros((8, NX), jnp.float32)


def pack_rates(feed, decay):
    return pallas(pack_rates_kernel, "pack_rates", 4, out_shape=vmem(RATE_ROWS, NX))(feed, decay)


def pack_y_kernel(u, v, feed, decay, x_b, x_a, out_b, out_a):
    even_x, even_y = is_even("gx"), is_even("gy")
    _, inner, _ = lanes()
    top = lax.broadcasted_iota(jnp.int32, (8, NX), 0) < 4
    starts = (jnp.where(even_y, OWN, OWN + 28), jnp.where(even_y, OWN + 28, OWN))
    rate_start = jnp.where(even_y, OWN + 29, OWN)

    def rows(z, carry):
        for out, start in zip((out_b, out_a), starts):
            out[pl.ds(FIELDS * z, 4), :] = u[z, pl.ds(start, 4), :]
            out[pl.ds(FIELDS * z + 4, 4), :] = v[z, pl.ds(start, 4), :]
        out_a[pl.ds(TAIL + RATES * z, 3), :] = feed[z, pl.ds(rate_start, 3), :]
        out_a[pl.ds(TAIL + RATES * z + 3, 3), :] = decay[z, pl.ds(rate_start, 3), :]
        return carry

    lax.fori_loop(0, NZ, rows, 0, unroll=4)
    out_a[pl.ds(TAIL + RATES * NZ, 8), :] = jnp.zeros((8, NX), jnp.float32)
    for j in range(GZ):
        made = []
        for first, base in ((0, 0), (4, 12)):
            sides = []
            for is_right in (True, False):
                value = None
                for n in range(4):
                    b, a = x_b[n, j], x_a[n, j]
                    halo = jnp.where(even_x, a, b) if is_right else jnp.where(even_x, b, a)
                    here = (inner >= 4 * n) & (inner < 4 * n + 4)
                    halo = turn(halo, 4 * n - base)
                    value = halo if n == 0 else jnp.where(here, halo, value)
                sides.append(turn(value, (0 if is_right else 4) - first, 0))
            made.append(jnp.where(top, sides[0], sides[1]))
        at = pl.ds(CORNER + 8 * j, 8)
        out_b[at, :] = jnp.where(even_y, made[0], made[1])
        out_a[at, :] = jnp.where(even_y, made[1], made[0])


def pack_y(u, v, feed, decay, x_b, x_a):
    return pallas(pack_y_kernel, "pack_y", 8, out_shape=(vmem(TAIL, NX), vmem(TAIL + RATE_ROWS, NX)))(
        u, v, feed, decay, x_b, x_a
    )


def x_sums(src_u, src_v, z, rows):
    sums = []
    for ref in (src_u, src_v):
        for row in rows:
            value = ref[z, pl.ds(row, 8), :]
            sums.append(turn(value, 1) + turn(value, -1))
    return tuple(sums)


def step_rows(src_u, src_v, feed, decay, z, below, above, row, x_u, x_v):
    at, down, up = pl.ds(row, 8), pl.ds(row - 1, 8), pl.ds(row + 1, 8)
    u, v, f = src_u[z, at, :], src_v[z, at, :], feed[z, at, :]
    near_u = x_u + (src_u[z, down, :] + src_u[z, up, :])
    near_v = x_v + (src_v[z, down, :] + src_v[z, up, :])
    along_u = src_u[below, at, :] + src_u[above, at, :]
    along_v = src_v[below, at, :] + src_v[above, at, :]
    react = u * (v * v)
    new_u = (0.24 * near_u + 0.01 * along_u) + (f - u * (f - 0.02)) - react
    new_v = (0.12 * near_v + 0.005 * along_v) + decay[z, at, :] * v + react
    return new_u, new_v


def sweep(src, rates, rows, count, place, emit, unroll):
    def body(i, sums):
        z, below, above = place(i)
        ahead = x_sums(*src, place(jnp.minimum(i + 1, count - 1))[0], rows)
        values = [
            step_rows(*src, *rates, z, below, above, row, sums[n], sums[len(rows) + n])
            for n, row in enumerate(rows)
        ]
        emit(z, values)
        return ahead

    lax.fori_loop(0, count, body, x_sums(*src, place(0)[0], rows), unroll=unroll)


def to_planes(dst, rows):
    def emit(z, values):
        for row, new in zip(rows, values):
            for ref, value in zip(dst, new):
                ref[z, pl.ds(row, 8), :] = value

    return emit


def main_place(i):
    return i, jnp.maximum(i - 1, 0), jnp.minimum(i + 1, NZ - 1)


def strip_place(i):
    z = jnp.where(i < GZ, i + RIGHT, i - GZ + LEFT)
    return z, z - 1, z + 1


def strip_ends(refs, rows, group):
    for ref in refs:
        for plane in (RIGHT, LEFT):
            for row in rows:
                at = pl.ds(row, 8)
                first, last = ref[plane, at, :], ref[plane + GZ - 1, at, :]
                ref[plane - 1, at, :] = jnp.where(group == 0, first, turn(last, 16))
                ref[plane + GZ, at, :] = jnp.where(group == GROUPS - 1, last, turn(first, -16))


def merge_strips(src, dst, rows, inner):
    for old, new in zip(src, dst):
        for j in range(GZ):
            for row in rows:
                at = pl.ds(row, 8)
                new[j, at, :] = jnp.where(inner < 8, old[j + RIGHT, at, :], old[j + LEFT, at, :])


def with_edges(merged, z, row, value, edge):
    g = lax.div(z, GZ)
    piece = merged[z - g * GZ, pl.ds(row, 8), :]
    return jnp.where(edge, pltpu.roll(piece, NX - 8 - 16 * g, 1), value)


INNER_ROWS = (8, 16, 24, 32)
LAST_INNER_ROWS = (12, 20, 28)
BORDER_ROWS = (4, 36)
LAST_BORDER_ROWS = (8, 36)


def interior_kernel(
    u0, v0, feed, decay, x_b, x_a, su0_in, sv0_in, s_feed_in, s_decay_in,
    su0, sv0, s_feed, s_decay, u1, v1, u2, v2, u3, v3, su1, sv1, su2, sv2, su3, sv3, o_u, o_v,
    su4, sv4, mu, mv,
):
    even_x = is_even("gx")
    lane, inner, group = lanes()
    right_halo = (inner >= 8) & (inner < 12)
    left_halo = (inner >= 4) & (inner < 8)

    def halos(j, carry):
        for n, ref in enumerate((su0, sv0, s_feed, s_decay)):
            b, a = x_b[n, j], x_a[n, j]
            on_right, on_left = jnp.where(even_x, a, b), jnp.where(even_x, b, a)
            for t in range(4):
                at = pl.ds(OWN + 8 * t, 8)
                both = ref[j + RIGHT, at, :]
                ref[j + RIGHT, at, :] = jnp.where(right_halo, turn(on_right, 8 - 4 * t), both)
                ref[j + LEFT, at, :] = jnp.where(left_halo, turn(on_left, 4 - 4 * t), both)
        return carry

    lax.fori_loop(0, GZ, halos, 0, unroll=True)

    levels = [(su0, sv0), (su1, sv1), (su2, sv2), (su3, sv3), (su4, sv4)]
    for step in range(STEPS):
        rows = INNER_ROWS if step < STEPS - 1 else LAST_INNER_ROWS
        strip_ends(levels[step], INNER_ROWS, group)
        emit = to_planes(levels[step + 1], rows)
        sweep(levels[step], (s_feed, s_decay), rows, 2 * GZ, strip_place, emit, 14)
    merge_strips((su4, sv4), (mu, mv), LAST_INNER_ROWS, inner)

    levels = [(u0, v0), (u1, v1), (u2, v2), (u3, v3)]
    for step in range(STEPS - 1):
        emit = to_planes(levels[step + 1], INNER_ROWS)
        sweep(levels[step], (feed, decay), INNER_ROWS, NZ, main_place, emit, 14)
    edge = (lane < 4) | (lane >= 124)

    def finish(z, values):
        for row, new in zip(LAST_INNER_ROWS, values):
            for out, merged, value in zip((o_u, o_v), (mu, mv), new):
                out[z, pl.ds(row - OWN, 8), :] = with_edges(merged, z, row, value, edge)

    sweep(levels[-1], (feed, decay), LAST_INNER_ROWS, NZ, main_place, finish, 14)


def interior(u0, v0, feed, decay, x_b, x_a, su0, sv0, s_feed, s_decay):
    out = (vmem(*STRIP),) * 4 + (vmem(*FIELD),) * 6 + (vmem(*STRIP),) * 6 + (vmem(NZ, NY, NX),) * 2
    return pallas(
        interior_kernel,
        "interior",
        4,
        40_000_000,
        out_shape=out,
        input_output_aliases={6: 0, 7: 1, 8: 2, 9: 3},
        scratch_shapes=[vmem(*STRIP)] * 2 + [vmem(GZ, PY, NX)] * 2,
    )(u0, v0, feed, decay, x_b, x_a, su0, sv0, s_feed, s_decay)


N_STATE = 22


def border_kernel(*refs):
    y_b, r_b, y_a = refs[:3]
    state = refs[3 + N_STATE : 3 + 2 * N_STATE]
    out_u, out_v, su4, sv4, mu, mv, sems = refs[3 + 2 * N_STATE :]
    (u0, v0, feed, decay, su0, sv0, s_feed, s_decay) = state[:8]
    (u1, v1, u2, v2, u3, v3, su1, sv1, su2, sv2, su3, sv3, o_u, o_v) = state[8:]
    even_y = is_even("gy")
    lane, inner, group = lanes()
    start = (jnp.where(even_y, LOW, HIGH), jnp.where(even_y, HIGH, LOW))
    rate_start = (jnp.where(even_y, LOW + 1, HIGH), jnp.where(even_y, HIGH, LOW + 1))

    sides = ((y_b, r_b, 0), (y_a, y_a, TAIL))

    def rows(z, carry):
        for (src, rate_src, tail), to, rate_to in zip(sides, start, rate_start):
            u0[z, pl.ds(to, 4), :] = src[pl.ds(FIELDS * z, 4), :]
            v0[z, pl.ds(to, 4), :] = src[pl.ds(FIELDS * z + 4, 4), :]
            feed[z, pl.ds(rate_to, 3), :] = rate_src[pl.ds(tail + RATES * z, 3), :]
            decay[z, pl.ds(rate_to, 3), :] = rate_src[pl.ds(tail + RATES * z + 3, 3), :]
        return carry

    lax.fori_loop(0, NZ, rows, 0, unroll=4)

    right_halo = (inner >= 8) & (inner < 12)
    left_halo = (inner >= 4) & (inner < 8)

    def strip(j, carry):
        for (y, rate_src, tail), to, rate_to in zip(sides, start, rate_start):
            fields = rates = None
            for g in range(GROUPS):
                z = GZ * g + j
                one = turn(y[pl.ds(FIELDS * z, 8), :], 16 * g + 8)
                two = turn(rate_src[pl.ds(tail + RATES * z, 8), :], 16 * g + 8)
                fields = one if g == 0 else jnp.where(group == g, one, fields)
                rates = two if g == 0 else jnp.where(group == g, two, rates)
            corner = y[pl.ds(CORNER + 8 * j, 8), :]
            other = turn(corner, 4, 0)
            for plane, mask, lane_at, top, bottom in (
                (j + RIGHT, right_halo, 8, corner, other),
                (j + LEFT, left_halo, 4, other, corner),
            ):
                su0[plane, pl.ds(to, 4), :] = jnp.where(mask, turn(top, lane_at), fields)[:4]
                sv0[plane, pl.ds(to, 4), :] = jnp.where(mask, turn(bottom, lane_at - 4), fields)[4:]
                s_feed[plane, pl.ds(rate_to, 3), :] = rates[:3]
                s_decay[plane, pl.ds(rate_to, 3), :] = rates[3:6]
                for n, ref in ((2, s_feed), (3, s_decay)):
                    halo = turn(top, lane_at - 4 * n)[:4]
                    at = pl.ds(to, 4)
                    ref[plane, at, :] = jnp.where(mask[:4], halo, ref[plane, at, :])
        return carry

    lax.fori_loop(0, GZ, strip, 0, unroll=True)

    levels = [(su0, sv0), (su1, sv1), (su2, sv2), (su3, sv3), (su4, sv4)]
    for step in range(STEPS):
        rows_now = BORDER_ROWS if step < STEPS - 1 else LAST_BORDER_ROWS
        strip_ends(levels[step], BORDER_ROWS, group)
        emit = to_planes(levels[step + 1], rows_now)
        sweep(levels[step], (s_feed, s_decay), rows_now, 2 * GZ, strip_place, emit, 14)
    merge_strips((su4, sv4), (mu, mv), LAST_BORDER_ROWS, inner)

    levels = [(u0, v0), (u1, v1), (u2, v2), (u3, v3)]
    for step in range(STEPS - 1):
        emit = to_planes(levels[step + 1], BORDER_ROWS)
        sweep(levels[step], (feed, decay), BORDER_ROWS, NZ, main_place, emit, 28)
    edge = (lane < 4) | (lane >= 124)

    def finish(z, values):
        for row, to, new in zip(LAST_BORDER_ROWS, (0, NY - 4), values):
            for out, merged, value in zip((o_u, o_v), (mu, mv), new):
                out[z, pl.ds(to, 4), :] = with_edges(merged, z, row, value, edge)[:4]

    copies = []
    part = NZ // 4
    for c in range(4):

        def place(i, c=c):
            return main_place(i + c * part)

        sweep(levels[-1], (feed, decay), LAST_BORDER_ROWS, part, place, finish, part)
        for n, (src, dst) in enumerate(((o_u, out_u), (o_v, out_v))):
            at = pl.ds(c * part, part)
            copies.append(pltpu.make_async_copy(src.at[at], dst.at[at], sems.at[2 * c + n]))
            copies[-1].start()
    for copy in copies:
        copy.wait()


def border(y_b, r_b, y_a, *state):
    out = tuple(vmem(*a.shape) for a in state) + (jax.ShapeDtypeStruct((NZ, NY, NX), jnp.float32),) * 2
    specs = [pl.BlockSpec(memory_space=pltpu.VMEM)] * N_STATE + [pl.BlockSpec(memory_space=pltpu.HBM)] * 2
    return pallas(
        border_kernel,
        "border",
        4,
        20_000_000,
        out_shape=out,
        out_specs=tuple(specs),
        input_output_aliases={3 + n: n for n in range(N_STATE)},
        scratch_shapes=[vmem(*STRIP)] * 2 + [vmem(GZ, PY, NX)] * 2 + [pltpu.SemaphoreType.DMA((8,))],
    )(y_b, r_b, y_a, *state)[N_STATE:]


def shards(activator, inhibitor, feed_rate, kill_rate):
    u0, v0, feed, decay, su0, sv0, s_feed, s_decay, x_send_b, x_send_a = load(
        activator, inhibitor, feed_rate, kill_rate
    )
    x_b = swap(x_send_b, "gx", 1)
    x_a = swap(x_send_a, "gx", 0)
    rates = pack_rates(feed, decay)
    half_way = relay(rates, "gy")
    x_b, x_a, _ = lax.optimization_barrier((x_b, x_a, rates))
    send_b, send_a = pack_y(u0, v0, feed, decay, x_b, x_a)
    y_b = swap(send_b, "gy", 1)
    send_a, half_way, x_b = lax.optimization_barrier((send_a, half_way, x_b))
    y_a = swap(send_a, "gy", 0)
    r_b = after_relay(half_way, "gy")
    made = interior(u0, v0, feed, decay, x_b, x_a, su0, sv0, s_feed, s_decay)
    return border(y_b, r_b, y_a, u0, v0, feed, decay, *made)


def solution(mesh):
    spec = P(None, "gy", "gx")
    return jax.shard_map(
        shards, mesh=mesh, in_specs=(spec,) * 4, out_specs=(spec,) * 2, check_vma=False
    )
```

```python
import functools

import jax
import jax.numpy as jnp
from jax import lax
from jax.experimental import pallas as pl
from jax.experimental.pallas import tpu as pltpu
from jax.sharding import PartitionSpec as P

STEPS = 4
NZ, NY, NX = 56, 32, 128
W = 4
PY = 48
OWN, LOW, HIGH = 8, 4, 40
GROUPS, GZ = 8, NZ // 8
FIELDS, RATES = 2 * W, 2 * (W - 1)
CORNER = NZ * FIELDS
TAIL = CORNER + 8 * GZ
RATE_ROWS = NZ * RATES + 8
RIGHT, LEFT = 1, GZ + 3
SPLANES = 2 * GZ + 4


def swap_pairs(count, parity):
    pairs = []
    for low in range(parity, count, 2):
        high = (low + 1) % count
        pairs += [(low, high), (high, low)]
    return pairs


def swap(block, axis, parity):
    return lax.ppermute(block, axis, swap_pairs(lax.axis_size(axis), parity))


SPAN = 8


def relay_pairs(count):
    pairs = []
    for i in range(count):
        run, place = divmod(i, SPAN)
        runs = count // SPAN
        step = {0: -1, SPAN - 1: 1}.get(place, 0)
        pairs.append((i, (run + step) % runs * SPAN + place))
    return pairs


def second_pairs(count):
    pairs = []
    for i in range(count):
        run, place = divmod(i, SPAN)
        other = (place + 1 if place % 2 else place - 1) % SPAN
        pairs.append((i, run * SPAN + other))
    return pairs


def relay(block, axis):
    count = lax.axis_size(axis)
    return lax.ppermute(block, axis, relay_pairs(count)) if count % SPAN == 0 else block


def after_relay(block, axis):
    count = lax.axis_size(axis)
    return lax.ppermute(block, axis, second_pairs(count) if count % SPAN == 0 else swap_pairs(count, 1))


def is_even(axis):
    return lax.rem(lax.axis_index(axis), 2) == 0


def lanes():
    lane = lax.broadcasted_iota(jnp.int32, (8, NX), 1)
    return lane, lax.rem(lane, 16), lax.div(lane, 16)


def turn(value, shift, axis=1):
    shift = shift % value.shape[axis]
    return value if shift == 0 else pltpu.roll(value, shift, axis)


def vmem(*shape):
    return pltpu.VMEM(shape, jnp.float32)


FIELD = (NZ, PY, NX)
STRIP = (SPLANES, PY, NX)
EDGE = (4, GZ, 8, NX)


def pallas(kernel, name, megabytes, flops=0, **kwargs):
    return pl.pallas_call(
        kernel,
        name=name,
        compiler_params=pltpu.CompilerParams(vmem_limit_bytes=megabytes * 1024 * 1024),
        cost_estimate=pl.CostEstimate(flops=flops, bytes_accessed=flops // 4, transcendentals=0),
        **kwargs,
    )


def load_kernel(u, v, f, k, pu, pv, feed, decay, su, sv, s_feed, s_decay, out_b, out_a, fs, ks, sems):
    own = pl.ds(OWN, NY)
    copies = [
        pltpu.make_async_copy(f, fs, sems.at[0]),
        pltpu.make_async_copy(k, ks, sems.at[1]),
        pltpu.make_async_copy(u, pu.at[:, own, :], sems.at[2]),
        pltpu.make_async_copy(v, pv.at[:, own, :], sems.at[3]),
    ]
    for copy in copies:
        copy.start()
    even = is_even("gx")
    _, inner, group = lanes()

    def rates(z, carry):
        for t in range(0, 4, 2):
            at, to = pl.ds(pl.multiple_of(z * NY, NY) + 8 * t, 16), pl.ds(OWN + 8 * t, 16)
            rate = fs[at, :].astype(jnp.float32)
            feed[z, to, :] = rate
            decay[z, to, :] = 0.51 - (rate + ks[at, :].astype(jnp.float32))
        return carry

    copies[0].wait()
    copies[1].wait()
    lax.fori_loop(0, NZ, rates, 0, unroll=4)

    def pack(arrays):
        def body(j, carry):
            for n, src, dst in arrays:
                left_edge = right_edge = None
                for t in range(4):
                    at = pl.ds(OWN + 8 * t, 8)
                    both = None
                    for g in range(GROUPS):
                        value = turn(src[GZ * g + j, at, :], 16 * g + 8)
                        both = value if g == 0 else jnp.where(group == g, value, both)
                    dst[j + RIGHT, at, :] = both
                    dst[j + LEFT, at, :] = both
                    low, high = turn(both, 4 * t - 8), turn(both, 4 * t - 4)
                    here = (inner >= 4 * t) & (inner < 4 * t + 4)
                    left_edge = low if t == 0 else jnp.where(here, low, left_edge)
                    right_edge = high if t == 0 else jnp.where(here, high, right_edge)
                out_b[n, j] = jnp.where(even, left_edge, right_edge)
                out_a[n, j] = jnp.where(even, right_edge, left_edge)
            return carry

        lax.fori_loop(0, GZ, body, 0, unroll=2)

    pack(((2, feed, s_feed), (3, decay, s_decay)))
    copies[2].wait()
    copies[3].wait()
    pack(((0, pu, su), (1, pv, sv)))


def load(u, v, f, k):
    f, k = f.reshape(NZ * NY, NX), k.reshape(NZ * NY, NX)
    u, v, f, k = (pltpu.with_memory_space_constraint(a, pltpu.HBM) for a in (u, v, f, k))
    rates = pltpu.VMEM((NZ * NY, NX), jnp.bfloat16)
    return pallas(
        load_kernel,
        "load",
        8,
        out_shape=(vmem(*FIELD),) * 4 + (vmem(*STRIP),) * 4 + (vmem(*EDGE),) * 2,
        in_specs=[pl.BlockSpec(memory_space=pltpu.HBM)] * 4,
        scratch_shapes=[rates, rates, pltpu.SemaphoreType.DMA((4,))],
    )(u, v, f, k)


def pack_rates_kernel(feed, decay, out):
    start = jnp.where(is_even("gy"), OWN, OWN + 29)

    def rows(z, carry):
        out[pl.ds(RATES * z, 3), :] = feed[z, pl.ds(start, 3), :]
        out[pl.ds(RATES * z + 3, 3), :] = decay[z, pl.ds(start, 3), :]
        return carry

    lax.fori_loop(0, NZ, rows, 0, unroll=8)
    out[pl.ds(RATES * NZ, 8), :] = jnp.zeros((8, NX), jnp.float32)


def pack_rates(feed, decay):
    return pallas(pack_rates_kernel, "pack_rates", 4, out_shape=vmem(RATE_ROWS, NX))(feed, decay)


def pack_y_kernel(which, u, v, feed, decay, x_b, x_a, _, out):
    even_x = is_even("gx")
    to_low = is_even("gy") if which else jnp.logical_not(is_even("gy"))
    inner = lanes()[1]
    top = lax.broadcasted_iota(jnp.int32, (8, NX), 0) < 4
    start, rate_start = jnp.where(to_low, OWN, OWN + 28), jnp.where(to_low, OWN, OWN + 29)

    def rows(z, carry):
        out[pl.ds(FIELDS * z, 4), :] = u[z, pl.ds(start, 4), :]
        out[pl.ds(FIELDS * z + 4, 4), :] = v[z, pl.ds(start, 4), :]
        if not which:
            out[pl.ds(TAIL + RATES * z, 3), :] = feed[z, pl.ds(rate_start, 3), :]
            out[pl.ds(TAIL + RATES * z + 3, 3), :] = decay[z, pl.ds(rate_start, 3), :]
        return carry

    lax.fori_loop(0, NZ, rows, 0, unroll=8)
    if not which:
        out[pl.ds(TAIL + RATES * NZ, 8), :] = jnp.zeros((8, NX), jnp.float32)

    def corner(j, carry):
        made = []
        for first, base in ((0, 0), (4, 12)):
            sides = []
            for is_right in (True, False):
                value = None
                for n in range(4):
                    b, a = x_b[n, j], x_a[n, j]
                    halo = jnp.where(even_x, a, b) if is_right else jnp.where(even_x, b, a)
                    here = (inner >= 4 * n) & (inner < 4 * n + 4)
                    halo = turn(halo, 4 * n - base)
                    value = halo if n == 0 else jnp.where(here, halo, value)
                sides.append(turn(value, (0 if is_right else 4) - first, 0))
            made.append(jnp.where(top, sides[0], sides[1]))
        out[pl.ds(CORNER + 8 * j, 8), :] = jnp.where(to_low, made[0], made[1])
        return carry

    lax.fori_loop(0, GZ, corner, 0, unroll=True)


def pack_y(which, u, v, feed, decay, x_b, x_a, after):
    return pallas(
        functools.partial(pack_y_kernel, which),
        "pack_odd" if which else "pack_even",
        8,
        out_shape=vmem(TAIL + (0 if which else RATE_ROWS), NX),
        in_specs=[pl.BlockSpec(memory_space=pltpu.VMEM)] * 6 + [pl.BlockSpec(memory_space=pl.ANY)],
    )(u, v, feed, decay, x_b, x_a, after)


def x_sums(src_u, src_v, z, rows):
    sums = []
    for ref in (src_u, src_v):
        for row in rows:
            value = ref[z, pl.ds(row, 8), :]
            sums.append(turn(value, 1) + turn(value, -1))
    return tuple(sums)


def step_rows(src_u, src_v, feed, decay, z, below, above, row, x_u, x_v):
    at, down, up = pl.ds(row, 8), pl.ds(row - 1, 8), pl.ds(row + 1, 8)
    u, v, f = src_u[z, at, :], src_v[z, at, :], feed[z, at, :]
    near_u = x_u + (src_u[z, down, :] + src_u[z, up, :])
    near_v = x_v + (src_v[z, down, :] + src_v[z, up, :])
    along_u = src_u[below, at, :] + src_u[above, at, :]
    along_v = src_v[below, at, :] + src_v[above, at, :]
    react = u * (v * v)
    new_u = (0.24 * near_u + 0.01 * along_u) + (f - u * (f - 0.02)) - react
    new_v = (0.12 * near_v + 0.005 * along_v) + decay[z, at, :] * v + react
    return new_u, new_v


def sweep(src, rates, rows, count, place, emit, unroll):
    def body(i, sums):
        z, below, above = place(i)
        ahead = x_sums(*src, place(jnp.minimum(i + 1, count - 1))[0], rows)
        values = [
            step_rows(*src, *rates, z, below, above, row, sums[n], sums[len(rows) + n])
            for n, row in enumerate(rows)
        ]
        emit(z, values)
        return ahead

    lax.fori_loop(0, count, body, x_sums(*src, place(0)[0], rows), unroll=unroll)


def to_planes(dst, rows):
    def emit(z, values):
        for row, new in zip(rows, values):
            for ref, value in zip(dst, new):
                ref[z, pl.ds(row, 8), :] = value

    return emit


def main_place(i):
    return i, jnp.maximum(i - 1, 0), jnp.minimum(i + 1, NZ - 1)


def strip_place(i):
    z = jnp.where(i < GZ, i + RIGHT, i - GZ + LEFT)
    return z, z - 1, z + 1


def strip_ends(refs, rows, group):
    for ref in refs:
        for plane in (RIGHT, LEFT):
            for row in rows:
                at = pl.ds(row, 8)
                first, last = ref[plane, at, :], ref[plane + GZ - 1, at, :]
                ref[plane - 1, at, :] = jnp.where(group == 0, first, turn(last, 16))
                ref[plane + GZ, at, :] = jnp.where(group == GROUPS - 1, last, turn(first, -16))


def merge_strips(src, dst, rows, inner):
    for old, new in zip(src, dst):
        for j in range(GZ):
            for row in rows:
                at = pl.ds(row, 8)
                new[j, at, :] = jnp.where(inner < 8, old[j + RIGHT, at, :], old[j + LEFT, at, :])


def with_edges(merged, z, row, value, edge):
    g = lax.div(z, GZ)
    piece = merged[z - g * GZ, pl.ds(row, 8), :]
    return jnp.where(edge, pltpu.roll(piece, NX - 8 - 16 * g, 1), value)


INNER_ROWS = (8, 16, 24, 32)
LAST_INNER_ROWS = (12, 20, 28)
BORDER_ROWS = (4, 36)
LAST_BORDER_ROWS = (8, 36)


def interior_kernel(
    u0, v0, feed, decay, x_b, x_a, su0_in, sv0_in, s_feed_in, s_decay_in,
    su0, sv0, s_feed, s_decay, u1, v1, u2, v2, u3, v3, su1, sv1, su2, sv2, su3, sv3, o_u, o_v,
    su4, sv4, mu, mv,
):
    even_x = is_even("gx")
    lane, inner, group = lanes()
    right_halo = (inner >= 8) & (inner < 12)
    left_halo = (inner >= 4) & (inner < 8)

    def halos(j, carry):
        for n, ref in enumerate((su0, sv0, s_feed, s_decay)):
            b, a = x_b[n, j], x_a[n, j]
            on_right, on_left = jnp.where(even_x, a, b), jnp.where(even_x, b, a)
            for t in range(4):
                at = pl.ds(OWN + 8 * t, 8)
                both = ref[j + RIGHT, at, :]
                ref[j + RIGHT, at, :] = jnp.where(right_halo, turn(on_right, 8 - 4 * t), both)
                ref[j + LEFT, at, :] = jnp.where(left_halo, turn(on_left, 4 - 4 * t), both)
        return carry

    lax.fori_loop(0, GZ, halos, 0, unroll=True)

    levels = [(su0, sv0), (su1, sv1), (su2, sv2), (su3, sv3), (su4, sv4)]
    for step in range(STEPS):
        rows = INNER_ROWS if step < STEPS - 1 else LAST_INNER_ROWS
        strip_ends(levels[step], INNER_ROWS, group)
        emit = to_planes(levels[step + 1], rows)
        sweep(levels[step], (s_feed, s_decay), rows, 2 * GZ, strip_place, emit, 14)
    merge_strips((su4, sv4), (mu, mv), LAST_INNER_ROWS, inner)

    levels = [(u0, v0), (u1, v1), (u2, v2), (u3, v3)]
    for step in range(STEPS - 1):
        emit = to_planes(levels[step + 1], INNER_ROWS)
        sweep(levels[step], (feed, decay), INNER_ROWS, NZ, main_place, emit, 14)
    edge = (lane < 4) | (lane >= 124)

    def finish(z, values):
        for row, new in zip(LAST_INNER_ROWS, values):
            for out, merged, value in zip((o_u, o_v), (mu, mv), new):
                out[z, pl.ds(row - OWN, 8), :] = with_edges(merged, z, row, value, edge)

    sweep(levels[-1], (feed, decay), LAST_INNER_ROWS, NZ, main_place, finish, 14)


def interior(u0, v0, feed, decay, x_b, x_a, su0, sv0, s_feed, s_decay):
    out = (vmem(*STRIP),) * 4 + (vmem(*FIELD),) * 6 + (vmem(*STRIP),) * 6 + (vmem(NZ, NY, NX),) * 2
    return pallas(
        interior_kernel,
        "interior",
        4,
        40_000_000_000,
        out_shape=out,
        input_output_aliases={6: 0, 7: 1, 8: 2, 9: 3},
        scratch_shapes=[vmem(*STRIP)] * 2 + [vmem(GZ, PY, NX)] * 2,
    )(u0, v0, feed, decay, x_b, x_a, su0, sv0, s_feed, s_decay)


N_STATE = 22


def border_kernel(*refs):
    y_b, r_b, y_a = refs[:3]
    state = refs[3 + N_STATE : 3 + 2 * N_STATE]
    out_u, out_v, su4, sv4, mu, mv, sems = refs[3 + 2 * N_STATE :]
    (u0, v0, feed, decay, su0, sv0, s_feed, s_decay) = state[:8]
    (u1, v1, u2, v2, u3, v3, su1, sv1, su2, sv2, su3, sv3, o_u, o_v) = state[8:]
    even_y = is_even("gy")
    lane, inner, group = lanes()
    start = (jnp.where(even_y, LOW, HIGH), jnp.where(even_y, HIGH, LOW))
    rate_start = (jnp.where(even_y, LOW + 1, HIGH), jnp.where(even_y, HIGH, LOW + 1))

    sides = ((y_b, r_b, 0), (y_a, y_a, TAIL))

    def rows(z, carry):
        for (src, rate_src, tail), to, rate_to in zip(sides, start, rate_start):
            u0[z, pl.ds(to, 4), :] = src[pl.ds(FIELDS * z, 4), :]
            v0[z, pl.ds(to, 4), :] = src[pl.ds(FIELDS * z + 4, 4), :]
            feed[z, pl.ds(rate_to, 3), :] = rate_src[pl.ds(tail + RATES * z, 3), :]
            decay[z, pl.ds(rate_to, 3), :] = rate_src[pl.ds(tail + RATES * z + 3, 3), :]
        return carry

    lax.fori_loop(0, NZ, rows, 0, unroll=4)

    right_halo = (inner >= 8) & (inner < 12)
    left_halo = (inner >= 4) & (inner < 8)

    def strip(j, carry):
        for (y, rate_src, tail), to, rate_to in zip(sides, start, rate_start):
            fields = rates = None
            for g in range(GROUPS):
                z = GZ * g + j
                one = turn(y[pl.ds(FIELDS * z, 8), :], 16 * g + 8)
                two = turn(rate_src[pl.ds(tail + RATES * z, 8), :], 16 * g + 8)
                fields = one if g == 0 else jnp.where(group == g, one, fields)
                rates = two if g == 0 else jnp.where(group == g, two, rates)
            corner = y[pl.ds(CORNER + 8 * j, 8), :]
            other = turn(corner, 4, 0)
            for plane, mask, lane_at, top, bottom in (
                (j + RIGHT, right_halo, 8, corner, other),
                (j + LEFT, left_halo, 4, other, corner),
            ):
                su0[plane, pl.ds(to, 4), :] = jnp.where(mask, turn(top, lane_at), fields)[:4]
                sv0[plane, pl.ds(to, 4), :] = jnp.where(mask, turn(bottom, lane_at - 4), fields)[4:]
                s_feed[plane, pl.ds(rate_to, 3), :] = rates[:3]
                s_decay[plane, pl.ds(rate_to, 3), :] = rates[3:6]
                for n, ref in ((2, s_feed), (3, s_decay)):
                    halo = turn(top, lane_at - 4 * n)[:4]
                    at = pl.ds(to, 4)
                    ref[plane, at, :] = jnp.where(mask[:4], halo, ref[plane, at, :])
        return carry

    lax.fori_loop(0, GZ, strip, 0, unroll=True)

    levels = [(su0, sv0), (su1, sv1), (su2, sv2), (su3, sv3), (su4, sv4)]
    for step in range(STEPS):
        rows_now = BORDER_ROWS if step < STEPS - 1 else LAST_BORDER_ROWS
        strip_ends(levels[step], BORDER_ROWS, group)
        emit = to_planes(levels[step + 1], rows_now)
        sweep(levels[step], (s_feed, s_decay), rows_now, 2 * GZ, strip_place, emit, 14)
    merge_strips((su4, sv4), (mu, mv), LAST_BORDER_ROWS, inner)

    levels = [(u0, v0), (u1, v1), (u2, v2), (u3, v3)]
    for step in range(STEPS - 1):
        emit = to_planes(levels[step + 1], BORDER_ROWS)
        sweep(levels[step], (feed, decay), BORDER_ROWS, NZ, main_place, emit, 28)
    edge = (lane < 4) | (lane >= 124)

    def finish(z, values):
        for row, to, new in zip(LAST_BORDER_ROWS, (0, NY - 4), values):
            for out, merged, value in zip((o_u, o_v), (mu, mv), new):
                out[z, pl.ds(to, 4), :] = with_edges(merged, z, row, value, edge)[:4]

    copies = []
    part = NZ // 4
    for c in range(4):

        def place(i, c=c):
            return main_place(i + c * part)

        sweep(levels[-1], (feed, decay), LAST_BORDER_ROWS, part, place, finish, part)
        for n, (src, dst) in enumerate(((o_u, out_u), (o_v, out_v))):
            at = pl.ds(c * part, part)
            copies.append(pltpu.make_async_copy(src.at[at], dst.at[at], sems.at[2 * c + n]))
            copies[-1].start()
    for copy in copies:
        copy.wait()


def border(y_b, r_b, y_a, *state):
    out = tuple(vmem(*a.shape) for a in state) + (jax.ShapeDtypeStruct((NZ, NY, NX), jnp.float32),) * 2
    specs = [pl.BlockSpec(memory_space=pltpu.VMEM)] * N_STATE + [pl.BlockSpec(memory_space=pltpu.HBM)] * 2
    return pallas(
        border_kernel,
        "border",
        4,
        20_000_000,
        out_shape=out,
        out_specs=tuple(specs),
        input_output_aliases={3 + n: n for n in range(N_STATE)},
        scratch_shapes=[vmem(*STRIP)] * 2 + [vmem(GZ, PY, NX)] * 2 + [pltpu.SemaphoreType.DMA((8,))],
    )(y_b, r_b, y_a, *state)[N_STATE:]


def shards(activator, inhibitor, feed_rate, kill_rate):
    u0, v0, feed, decay, su0, sv0, s_feed, s_decay, x_send_b, x_send_a = load(
        activator, inhibitor, feed_rate, kill_rate
    )
    x_b = swap(x_send_b, "gx", 1)
    x_a = swap(x_send_a, "gx", 0)
    rates, x_b, x_a = lax.optimization_barrier((pack_rates(feed, decay), x_b, x_a))
    half_way = relay(rates, "gy")
    send_b = pack_y(1, u0, v0, feed, decay, x_b, x_a, rates)
    y_b = swap(send_b, "gy", 1)
    send_a = pack_y(0, u0, v0, feed, decay, x_b, x_a, send_b)
    y_a = swap(send_a, "gy", 0)
    half_way, x_b, _ = lax.optimization_barrier((half_way, x_b, send_a))
    r_b = after_relay(half_way, "gy")
    made = interior(u0, v0, feed, decay, x_b, x_a, su0, sv0, s_feed, s_decay)
    return border(y_b, r_b, y_a, u0, v0, feed, decay, *made)


def solution(mesh):
    spec = P(None, "gy", "gx")
    return jax.shard_map(
        shards, mesh=mesh, in_specs=(spec,) * 4, out_specs=(spec,) * 2, check_vma=False
    )
```

```python
import functools

import jax
import jax.numpy as jnp
from jax import lax
from jax.experimental import pallas as pl
from jax.experimental.pallas import tpu as pltpu
from jax.sharding import PartitionSpec as P

STEPS = 4
NZ, NY, NX = 56, 32, 128
W = 4
PY = 48
OWN, LOW, HIGH = 8, 4, 40
GROUPS, GZ = 8, NZ // 8
FIELDS, RATES = 2 * W, 2 * (W - 1)
CORNER = NZ * FIELDS
TAIL = CORNER + 8 * GZ
RATE_ROWS = NZ * RATES + 8
RIGHT, LEFT = 1, GZ + 3
SPLANES = 2 * GZ + 4


def swap_pairs(count, parity):
    pairs = []
    for low in range(parity, count, 2):
        high = (low + 1) % count
        pairs += [(low, high), (high, low)]
    return pairs


def swap(block, axis, parity):
    return lax.ppermute(block, axis, swap_pairs(lax.axis_size(axis), parity))


SPAN = 8


def relay_pairs(count):
    pairs = []
    for i in range(count):
        run, place = divmod(i, SPAN)
        runs = count // SPAN
        step = {0: -1, SPAN - 1: 1}.get(place, 0)
        pairs.append((i, (run + step) % runs * SPAN + place))
    return pairs


def second_pairs(count):
    pairs = []
    for i in range(count):
        run, place = divmod(i, SPAN)
        other = (place + 1 if place % 2 else place - 1) % SPAN
        pairs.append((i, run * SPAN + other))
    return pairs


def relay(block, axis):
    count = lax.axis_size(axis)
    return lax.ppermute(block, axis, relay_pairs(count)) if count % SPAN == 0 else block


def after_relay(block, axis):
    count = lax.axis_size(axis)
    return lax.ppermute(block, axis, second_pairs(count) if count % SPAN == 0 else swap_pairs(count, 1))


def is_even(axis):
    return lax.rem(lax.axis_index(axis), 2) == 0


def lanes():
    lane = lax.broadcasted_iota(jnp.int32, (8, NX), 1)
    return lane, lax.rem(lane, 16), lax.div(lane, 16)


def turn(value, shift, axis=1):
    shift = shift % value.shape[axis]
    return value if shift == 0 else pltpu.roll(value, shift, axis)


def vmem(*shape):
    return pltpu.VMEM(shape, jnp.float32)


FIELD = (NZ, PY, NX)
STRIP = (SPLANES, PY, NX)
EDGE = (4, GZ, 8, NX)


def pallas(kernel, name, megabytes, flops=0, **kwargs):
    return pl.pallas_call(
        kernel,
        name=name,
        compiler_params=pltpu.CompilerParams(vmem_limit_bytes=megabytes * 1024 * 1024),
        cost_estimate=pl.CostEstimate(flops=flops, bytes_accessed=flops // 4, transcendentals=0),
        **kwargs,
    )


def load_kernel(u, v, f, k, pu, pv, feed, decay, su, sv, s_feed, s_decay, out_b, out_a, fs, ks, sems):
    own = pl.ds(OWN, NY)
    copies = [
        pltpu.make_async_copy(f, fs, sems.at[0]),
        pltpu.make_async_copy(k, ks, sems.at[1]),
        pltpu.make_async_copy(u, pu.at[:, own, :], sems.at[2]),
        pltpu.make_async_copy(v, pv.at[:, own, :], sems.at[3]),
    ]
    for copy in copies:
        copy.start()
    even = is_even("gx")
    _, inner, group = lanes()

    def rates(z, carry):
        for t in range(0, 4, 2):
            at, to = pl.ds(pl.multiple_of(z * NY, NY) + 8 * t, 16), pl.ds(OWN + 8 * t, 16)
            rate = fs[at, :].astype(jnp.float32)
            feed[z, to, :] = rate
            decay[z, to, :] = 0.51 - (rate + ks[at, :].astype(jnp.float32))
        return carry

    copies[0].wait()
    copies[1].wait()
    lax.fori_loop(0, NZ, rates, 0, unroll=4)

    def pack(arrays):
        def body(j, carry):
            for n, src, dst in arrays:
                left_edge = right_edge = None
                for t in range(4):
                    at = pl.ds(OWN + 8 * t, 8)
                    both = None
                    for g in range(GROUPS):
                        value = turn(src[GZ * g + j, at, :], 16 * g + 8)
                        both = value if g == 0 else jnp.where(group == g, value, both)
                    dst[j + RIGHT, at, :] = both
                    dst[j + LEFT, at, :] = both
                    low, high = turn(both, 4 * t - 8), turn(both, 4 * t - 4)
                    here = (inner >= 4 * t) & (inner < 4 * t + 4)
                    left_edge = low if t == 0 else jnp.where(here, low, left_edge)
                    right_edge = high if t == 0 else jnp.where(here, high, right_edge)
                out_b[n, j] = jnp.where(even, left_edge, right_edge)
                out_a[n, j] = jnp.where(even, right_edge, left_edge)
            return carry

        lax.fori_loop(0, GZ, body, 0, unroll=2)

    pack(((2, feed, s_feed), (3, decay, s_decay)))
    copies[2].wait()
    copies[3].wait()
    pack(((0, pu, su), (1, pv, sv)))


def load(u, v, f, k):
    f, k = f.reshape(NZ * NY, NX), k.reshape(NZ * NY, NX)
    u, v, f, k = (pltpu.with_memory_space_constraint(a, pltpu.HBM) for a in (u, v, f, k))
    rates = pltpu.VMEM((NZ * NY, NX), jnp.bfloat16)
    return pallas(
        load_kernel,
        "load",
        8,
        out_shape=(vmem(*FIELD),) * 4 + (vmem(*STRIP),) * 4 + (vmem(*EDGE),) * 2,
        in_specs=[pl.BlockSpec(memory_space=pltpu.HBM)] * 4,
        scratch_shapes=[rates, rates, pltpu.SemaphoreType.DMA((4,))],
    )(u, v, f, k)


def pack_rates_kernel(feed, decay, out):
    start = jnp.where(is_even("gy"), OWN, OWN + 29)

    def rows(z, carry):
        out[pl.ds(RATES * z, 3), :] = feed[z, pl.ds(start, 3), :]
        out[pl.ds(RATES * z + 3, 3), :] = decay[z, pl.ds(start, 3), :]
        return carry

    lax.fori_loop(0, NZ, rows, 0, unroll=8)
    out[pl.ds(RATES * NZ, 8), :] = jnp.zeros((8, NX), jnp.float32)


def pack_rates(feed, decay):
    return pallas(pack_rates_kernel, "pack_rates", 4, out_shape=vmem(RATE_ROWS, NX))(feed, decay)


def pack_y_kernel(which, u, v, feed, decay, x_b, x_a, _, out):
    even_x = is_even("gx")
    to_low = is_even("gy") if which else jnp.logical_not(is_even("gy"))
    inner = lanes()[1]
    top = lax.broadcasted_iota(jnp.int32, (8, NX), 0) < 4
    start, rate_start = jnp.where(to_low, OWN, OWN + 28), jnp.where(to_low, OWN, OWN + 29)

    def rows(z, carry):
        out[pl.ds(FIELDS * z, 4), :] = u[z, pl.ds(start, 4), :]
        out[pl.ds(FIELDS * z + 4, 4), :] = v[z, pl.ds(start, 4), :]
        if not which:
            out[pl.ds(TAIL + RATES * z, 3), :] = feed[z, pl.ds(rate_start, 3), :]
            out[pl.ds(TAIL + RATES * z + 3, 3), :] = decay[z, pl.ds(rate_start, 3), :]
        return carry

    lax.fori_loop(0, NZ, rows, 0, unroll=8)
    if not which:
        out[pl.ds(TAIL + RATES * NZ, 8), :] = jnp.zeros((8, NX), jnp.float32)

    def corner(j, carry):
        made = []
        for first, base in ((0, 0), (4, 12)):
            sides = []
            for is_right in (True, False):
                value = None
                for n in range(4):
                    b, a = x_b[n, j], x_a[n, j]
                    halo = jnp.where(even_x, a, b) if is_right else jnp.where(even_x, b, a)
                    here = (inner >= 4 * n) & (inner < 4 * n + 4)
                    halo = turn(halo, 4 * n - base)
                    value = halo if n == 0 else jnp.where(here, halo, value)
                sides.append(turn(value, (0 if is_right else 4) - first, 0))
            made.append(jnp.where(top, sides[0], sides[1]))
        out[pl.ds(CORNER + 8 * j, 8), :] = jnp.where(to_low, made[0], made[1])
        return carry

    lax.fori_loop(0, GZ, corner, 0, unroll=True)


def pack_y(which, u, v, feed, decay, x_b, x_a, after):
    return pallas(
        functools.partial(pack_y_kernel, which),
        "pack_odd" if which else "pack_even",
        8,
        out_shape=vmem(TAIL + (0 if which else RATE_ROWS), NX),
        in_specs=[pl.BlockSpec(memory_space=pltpu.VMEM)] * 6 + [pl.BlockSpec(memory_space=pl.ANY)],
    )(u, v, feed, decay, x_b, x_a, after)


def x_sums(src_u, src_v, z, rows):
    sums = []
    for ref in (src_u, src_v):
        for row in rows:
            value = ref[z, pl.ds(row, 8), :]
            sums.append(turn(value, 1) + turn(value, -1))
    return tuple(sums)


def step_rows(src_u, src_v, feed, decay, z, below, above, row, x_u, x_v):
    at, down, up = pl.ds(row, 8), pl.ds(row - 1, 8), pl.ds(row + 1, 8)
    u, v, f = src_u[z, at, :], src_v[z, at, :], feed[z, at, :]
    near_u = x_u + (src_u[z, down, :] + src_u[z, up, :])
    near_v = x_v + (src_v[z, down, :] + src_v[z, up, :])
    along_u = src_u[below, at, :] + src_u[above, at, :]
    along_v = src_v[below, at, :] + src_v[above, at, :]
    react = u * (v * v)
    new_u = (0.24 * near_u + 0.01 * along_u) + (f - u * (f - 0.02)) - react
    new_v = (0.12 * near_v + 0.005 * along_v) + decay[z, at, :] * v + react
    return new_u, new_v


def sweep(src, rates, rows, count, place, emit, unroll):
    def body(i, sums):
        z, below, above = place(i)
        ahead = x_sums(*src, place(jnp.minimum(i + 1, count - 1))[0], rows)
        values = [
            step_rows(*src, *rates, z, below, above, row, sums[n], sums[len(rows) + n])
            for n, row in enumerate(rows)
        ]
        emit(z, values)
        return ahead

    lax.fori_loop(0, count, body, x_sums(*src, place(0)[0], rows), unroll=unroll)


def to_planes(dst, rows):
    def emit(z, values):
        for row, new in zip(rows, values):
            for ref, value in zip(dst, new):
                ref[z, pl.ds(row, 8), :] = value

    return emit


def main_place(i):
    return i, jnp.maximum(i - 1, 0), jnp.minimum(i + 1, NZ - 1)


def strip_place(i):
    z = jnp.where(i < GZ, i + RIGHT, i - GZ + LEFT)
    return z, z - 1, z + 1


def strip_ends(refs, rows, group):
    for ref in refs:
        for plane in (RIGHT, LEFT):
            for row in rows:
                at = pl.ds(row, 8)
                first, last = ref[plane, at, :], ref[plane + GZ - 1, at, :]
                ref[plane - 1, at, :] = jnp.where(group == 0, first, turn(last, 16))
                ref[plane + GZ, at, :] = jnp.where(group == GROUPS - 1, last, turn(first, -16))


def merge_strips(src, dst, rows, inner):
    for old, new in zip(src, dst):
        for j in range(GZ):
            for row in rows:
                at = pl.ds(row, 8)
                new[j, at, :] = jnp.where(inner < 8, old[j + RIGHT, at, :], old[j + LEFT, at, :])


def with_edges(merged, z, row, value, edge):
    g = lax.div(z, GZ)
    piece = merged[z - g * GZ, pl.ds(row, 8), :]
    return jnp.where(edge, pltpu.roll(piece, NX - 8 - 16 * g, 1), value)


INNER_ROWS = (8, 16, 24, 32)
LAST_INNER_ROWS = (12, 20, 28)
BORDER_ROWS = (4, 36)
LAST_BORDER_ROWS = (8, 36)


EARLY_STEPS = 2


def early_kernel(
    u0, v0, feed, decay, x_b, x_a, su0_in, sv0_in, s_feed_in, s_decay_in,
    su0, sv0, s_feed, s_decay, su1, sv1, su2, sv2, su3, sv3, mu, mv, *fields_and_scratch,
):
    *fields, su4, sv4 = fields_and_scratch
    even_x = is_even("gx")
    lane, inner, group = lanes()
    right_halo = (inner >= 8) & (inner < 12)
    left_halo = (inner >= 4) & (inner < 8)

    def halos(j, carry):
        for n, ref in enumerate((su0, sv0, s_feed, s_decay)):
            b, a = x_b[n, j], x_a[n, j]
            on_right, on_left = jnp.where(even_x, a, b), jnp.where(even_x, b, a)
            for t in range(4):
                at = pl.ds(OWN + 8 * t, 8)
                both = ref[j + RIGHT, at, :]
                ref[j + RIGHT, at, :] = jnp.where(right_halo, turn(on_right, 8 - 4 * t), both)
                ref[j + LEFT, at, :] = jnp.where(left_halo, turn(on_left, 4 - 4 * t), both)
        return carry

    lax.fori_loop(0, GZ, halos, 0, unroll=True)

    levels = [(su0, sv0), (su1, sv1), (su2, sv2), (su3, sv3), (su4, sv4)]
    for step in range(STEPS):
        rows = INNER_ROWS if step < STEPS - 1 else LAST_INNER_ROWS
        strip_ends(levels[step], INNER_ROWS, group)
        emit = to_planes(levels[step + 1], rows)
        sweep(levels[step], (s_feed, s_decay), rows, 2 * GZ, strip_place, emit, 14)
    merge_strips((su4, sv4), (mu, mv), LAST_INNER_ROWS, inner)

    levels = [(u0, v0)] + list(zip(fields[::2], fields[1::2]))
    for step in range(EARLY_STEPS):
        emit = to_planes(levels[step + 1], INNER_ROWS)
        sweep(levels[step], (feed, decay), INNER_ROWS, NZ, main_place, emit, 14)


def early(u0, v0, feed, decay, x_b, x_a, su0, sv0, s_feed, s_decay):
    out = (vmem(*STRIP),) * 10 + (vmem(GZ, PY, NX),) * 2 + (vmem(*FIELD),) * (2 * EARLY_STEPS)
    return pallas(
        early_kernel,
        "early",
        4,
        20_000_000_000,
        out_shape=out,
        input_output_aliases={6: 0, 7: 1, 8: 2, 9: 3},
        scratch_shapes=[vmem(*STRIP)] * 2,
    )(u0, v0, feed, decay, x_b, x_a, su0, sv0, s_feed, s_decay)


def late_kernel(feed, decay, mu, mv, first_u, first_v, *outs):
    lane = lanes()[0]
    *fields, o_u, o_v = outs
    levels = [(first_u, first_v)] + list(zip(fields[::2], fields[1::2]))
    for step in range(STEPS - 1 - EARLY_STEPS):
        emit = to_planes(levels[step + 1], INNER_ROWS)
        sweep(levels[step], (feed, decay), INNER_ROWS, NZ, main_place, emit, 14)
    edge = (lane < 4) | (lane >= 124)

    def finish(z, values):
        for row, new in zip(LAST_INNER_ROWS, values):
            for out, merged, value in zip((o_u, o_v), (mu, mv), new):
                out[z, pl.ds(row - OWN, 8), :] = with_edges(merged, z, row, value, edge)

    sweep(levels[-1], (feed, decay), LAST_INNER_ROWS, NZ, main_place, finish, 14)


def late(feed, decay, mu, mv, first_u, first_v):
    out = (vmem(*FIELD),) * (2 * (STEPS - 1 - EARLY_STEPS)) + (vmem(NZ, NY, NX),) * 2
    return pallas(late_kernel, "late", 4, 20_000_000_000, out_shape=out)(feed, decay, mu, mv, first_u, first_v)


N_STATE = 22


def border_kernel(*refs):
    y_b, r_b, y_a = refs[:3]
    state = refs[3 + N_STATE : 3 + 2 * N_STATE]
    out_u, out_v, su4, sv4, mu, mv, sems = refs[3 + 2 * N_STATE :]
    (u0, v0, feed, decay, su0, sv0, s_feed, s_decay) = state[:8]
    (su1, sv1, su2, sv2, su3, sv3, u1, v1, u2, v2, u3, v3, o_u, o_v) = state[8:]
    even_y = is_even("gy")
    lane, inner, group = lanes()
    start = (jnp.where(even_y, LOW, HIGH), jnp.where(even_y, HIGH, LOW))
    rate_start = (jnp.where(even_y, LOW + 1, HIGH), jnp.where(even_y, HIGH, LOW + 1))

    sides = ((y_b, r_b, 0), (y_a, y_a, TAIL))

    def rows(z, carry):
        for (src, rate_src, tail), to, rate_to in zip(sides, start, rate_start):
            u0[z, pl.ds(to, 4), :] = src[pl.ds(FIELDS * z, 4), :]
            v0[z, pl.ds(to, 4), :] = src[pl.ds(FIELDS * z + 4, 4), :]
            feed[z, pl.ds(rate_to, 3), :] = rate_src[pl.ds(tail + RATES * z, 3), :]
            decay[z, pl.ds(rate_to, 3), :] = rate_src[pl.ds(tail + RATES * z + 3, 3), :]
        return carry

    lax.fori_loop(0, NZ, rows, 0, unroll=4)

    right_halo = (inner >= 8) & (inner < 12)
    left_halo = (inner >= 4) & (inner < 8)

    def strip(j, carry):
        for (y, rate_src, tail), to, rate_to in zip(sides, start, rate_start):
            fields = rates = None
            for g in range(GROUPS):
                z = GZ * g + j
                one = turn(y[pl.ds(FIELDS * z, 8), :], 16 * g + 8)
                two = turn(rate_src[pl.ds(tail + RATES * z, 8), :], 16 * g + 8)
                fields = one if g == 0 else jnp.where(group == g, one, fields)
                rates = two if g == 0 else jnp.where(group == g, two, rates)
            corner = y[pl.ds(CORNER + 8 * j, 8), :]
            other = turn(corner, 4, 0)
            for plane, mask, lane_at, top, bottom in (
                (j + RIGHT, right_halo, 8, corner, other),
                (j + LEFT, left_halo, 4, other, corner),
            ):
                su0[plane, pl.ds(to, 4), :] = jnp.where(mask, turn(top, lane_at), fields)[:4]
                sv0[plane, pl.ds(to, 4), :] = jnp.where(mask, turn(bottom, lane_at - 4), fields)[4:]
                s_feed[plane, pl.ds(rate_to, 3), :] = rates[:3]
                s_decay[plane, pl.ds(rate_to, 3), :] = rates[3:6]
                for n, ref in ((2, s_feed), (3, s_decay)):
                    halo = turn(top, lane_at - 4 * n)[:4]
                    at = pl.ds(to, 4)
                    ref[plane, at, :] = jnp.where(mask[:4], halo, ref[plane, at, :])
        return carry

    lax.fori_loop(0, GZ, strip, 0, unroll=True)

    levels = [(su0, sv0), (su1, sv1), (su2, sv2), (su3, sv3), (su4, sv4)]
    for step in range(STEPS):
        rows_now = BORDER_ROWS if step < STEPS - 1 else LAST_BORDER_ROWS
        strip_ends(levels[step], BORDER_ROWS, group)
        emit = to_planes(levels[step + 1], rows_now)
        sweep(levels[step], (s_feed, s_decay), rows_now, 2 * GZ, strip_place, emit, 14)
    merge_strips((su4, sv4), (mu, mv), LAST_BORDER_ROWS, inner)

    levels = [(u0, v0), (u1, v1), (u2, v2), (u3, v3)]
    for step in range(STEPS - 1):
        emit = to_planes(levels[step + 1], BORDER_ROWS)
        sweep(levels[step], (feed, decay), BORDER_ROWS, NZ, main_place, emit, 28)
    edge = (lane < 4) | (lane >= 124)

    def finish(z, values):
        for row, to, new in zip(LAST_BORDER_ROWS, (0, NY - 4), values):
            for out, merged, value in zip((o_u, o_v), (mu, mv), new):
                out[z, pl.ds(to, 4), :] = with_edges(merged, z, row, value, edge)[:4]

    copies = []
    part = NZ // 4
    for c in range(4):

        def place(i, c=c):
            return main_place(i + c * part)

        sweep(levels[-1], (feed, decay), LAST_BORDER_ROWS, part, place, finish, part)
        for n, (src, dst) in enumerate(((o_u, out_u), (o_v, out_v))):
            at = pl.ds(c * part, part)
            copies.append(pltpu.make_async_copy(src.at[at], dst.at[at], sems.at[2 * c + n]))
            copies[-1].start()
    for copy in copies:
        copy.wait()


def border(y_b, r_b, y_a, *state):
    out = tuple(vmem(*a.shape) for a in state) + (jax.ShapeDtypeStruct((NZ, NY, NX), jnp.float32),) * 2
    specs = [pl.BlockSpec(memory_space=pltpu.VMEM)] * N_STATE + [pl.BlockSpec(memory_space=pltpu.HBM)] * 2
    return pallas(
        border_kernel,
        "border",
        4,
        20_000_000,
        out_shape=out,
        out_specs=tuple(specs),
        input_output_aliases={3 + n: n for n in range(N_STATE)},
        scratch_shapes=[vmem(*STRIP)] * 2 + [vmem(GZ, PY, NX)] * 2 + [pltpu.SemaphoreType.DMA((8,))],
    )(y_b, r_b, y_a, *state)[N_STATE:]


def shards(activator, inhibitor, feed_rate, kill_rate):
    u0, v0, feed, decay, su0, sv0, s_feed, s_decay, x_send_b, x_send_a = load(
        activator, inhibitor, feed_rate, kill_rate
    )
    x_b = swap(x_send_b, "gx", 1)
    x_a = swap(x_send_a, "gx", 0)
    rates, x_b, x_a = lax.optimization_barrier((pack_rates(feed, decay), x_b, x_a))
    half_way = relay(rates, "gy")
    send_b = pack_y(1, u0, v0, feed, decay, x_b, x_a, rates)
    y_b = swap(send_b, "gy", 1)
    send_a = pack_y(0, u0, v0, feed, decay, x_b, x_a, send_b)
    y_a = swap(send_a, "gy", 0)
    x_b, _ = lax.optimization_barrier((x_b, send_a))
    made = early(u0, v0, feed, decay, x_b, x_a, su0, sv0, s_feed, s_decay)
    strips, (mu, mv), fields = made[:10], made[10:12], made[12:]
    half_way, mu = lax.optimization_barrier((half_way, mu))
    r_b = after_relay(half_way, "gy")
    rest = late(feed, decay, mu, mv, *fields[-2:])
    return border(y_b, r_b, y_a, u0, v0, feed, decay, *strips, *fields, *rest)


def solution(mesh):
    spec = P(None, "gy", "gx")
    return jax.shard_map(
        shards, mesh=mesh, in_specs=(spec,) * 4, out_specs=(spec,) * 2, check_vma=False
    )
```

```python
import functools

import jax
import jax.numpy as jnp
from jax import lax
from jax.experimental import pallas as pl
from jax.experimental.pallas import tpu as pltpu
from jax.sharding import PartitionSpec as P

STEPS = 4
NZ, NY, NX = 56, 32, 128
W = 4
PY = 48
OWN, LOW, HIGH = 8, 4, 40
GROUPS, GZ = 8, NZ // 8
FIELDS, RATES = 2 * W, 2 * (W - 1)
CORNER = NZ * FIELDS
TAIL = CORNER + 8 * GZ
RATE_ROWS = NZ * RATES + 8
RIGHT, LEFT = 1, GZ + 3
SPLANES = 2 * GZ + 4


def swap_pairs(count, parity):
    pairs = []
    for low in range(parity, count, 2):
        high = (low + 1) % count
        pairs += [(low, high), (high, low)]
    return pairs


def swap(block, axis, parity):
    return lax.ppermute(block, axis, swap_pairs(lax.axis_size(axis), parity))


SPAN = 8


def relay_pairs(count):
    pairs = []
    for i in range(count):
        run, place = divmod(i, SPAN)
        runs = count // SPAN
        step = {0: -1, SPAN - 1: 1}.get(place, 0)
        pairs.append((i, (run + step) % runs * SPAN + place))
    return pairs


def second_pairs(count):
    pairs = []
    for i in range(count):
        run, place = divmod(i, SPAN)
        other = (place + 1 if place % 2 else place - 1) % SPAN
        pairs.append((i, run * SPAN + other))
    return pairs


def relay(block, axis):
    count = lax.axis_size(axis)
    return lax.ppermute(block, axis, relay_pairs(count)) if count % SPAN == 0 else block


def after_relay(block, axis):
    count = lax.axis_size(axis)
    return lax.ppermute(block, axis, second_pairs(count) if count % SPAN == 0 else swap_pairs(count, 1))


def is_even(axis):
    return lax.rem(lax.axis_index(axis), 2) == 0


def lanes():
    lane = lax.broadcasted_iota(jnp.int32, (8, NX), 1)
    return lane, lax.rem(lane, 16), lax.div(lane, 16)


def turn(value, shift, axis=1):
    shift = shift % value.shape[axis]
    return value if shift == 0 else pltpu.roll(value, shift, axis)


def vmem(*shape):
    return pltpu.VMEM(shape, jnp.float32)


FIELD = (NZ, PY, NX)
STRIP = (SPLANES, PY, NX)
EDGE = (4, GZ, 8, NX)


def pallas(kernel, name, megabytes, flops=0, **kwargs):
    return pl.pallas_call(
        kernel,
        name=name,
        compiler_params=pltpu.CompilerParams(vmem_limit_bytes=megabytes * 1024 * 1024),
        cost_estimate=pl.CostEstimate(flops=flops, bytes_accessed=flops // 4, transcendentals=0),
        **kwargs,
    )


def load_kernel(u, v, f, k, pu, pv, feed, decay, su, sv, s_feed, s_decay, out_b, out_a, fs, ks, sems):
    own = pl.ds(OWN, NY)
    copies = [
        pltpu.make_async_copy(f, fs, sems.at[0]),
        pltpu.make_async_copy(k, ks, sems.at[1]),
        pltpu.make_async_copy(u, pu.at[:, own, :], sems.at[2]),
        pltpu.make_async_copy(v, pv.at[:, own, :], sems.at[3]),
    ]
    for copy in copies:
        copy.start()
    even = is_even("gx")
    _, inner, group = lanes()

    def rates(z, carry):
        for t in range(0, 4, 2):
            at, to = pl.ds(pl.multiple_of(z * NY, NY) + 8 * t, 16), pl.ds(OWN + 8 * t, 16)
            rate = fs[at, :].astype(jnp.float32)
            feed[z, to, :] = rate
            decay[z, to, :] = 0.51 - (rate + ks[at, :].astype(jnp.float32))
        return carry

    copies[0].wait()
    copies[1].wait()
    lax.fori_loop(0, NZ, rates, 0, unroll=4)

    def pack(arrays):
        def body(j, carry):
            for n, src, dst in arrays:
                left_edge = right_edge = None
                for t in range(4):
                    at = pl.ds(OWN + 8 * t, 8)
                    both = None
                    for g in range(GROUPS):
                        value = turn(src[GZ * g + j, at, :], 16 * g + 8)
                        both = value if g == 0 else jnp.where(group == g, value, both)
                    dst[j + RIGHT, at, :] = both
                    dst[j + LEFT, at, :] = both
                    low, high = turn(both, 4 * t - 8), turn(both, 4 * t - 4)
                    here = (inner >= 4 * t) & (inner < 4 * t + 4)
                    left_edge = low if t == 0 else jnp.where(here, low, left_edge)
                    right_edge = high if t == 0 else jnp.where(here, high, right_edge)
                out_b[n, j] = jnp.where(even, left_edge, right_edge)
                out_a[n, j] = jnp.where(even, right_edge, left_edge)
            return carry

        lax.fori_loop(0, GZ, body, 0, unroll=2)

    pack(((2, feed, s_feed), (3, decay, s_decay)))
    copies[2].wait()
    copies[3].wait()
    pack(((0, pu, su), (1, pv, sv)))


def load(u, v, f, k):
    f, k = f.reshape(NZ * NY, NX), k.reshape(NZ * NY, NX)
    u, v, f, k = (pltpu.with_memory_space_constraint(a, pltpu.HBM) for a in (u, v, f, k))
    rates = pltpu.VMEM((NZ * NY, NX), jnp.bfloat16)
    return pallas(
        load_kernel,
        "load",
        8,
        out_shape=(vmem(*FIELD),) * 4 + (vmem(*STRIP),) * 4 + (vmem(*EDGE),) * 2,
        in_specs=[pl.BlockSpec(memory_space=pltpu.HBM)] * 4,
        scratch_shapes=[rates, rates, pltpu.SemaphoreType.DMA((4,))],
    )(u, v, f, k)


def pack_rates_kernel(feed, decay, out):
    start = jnp.where(is_even("gy"), OWN, OWN + 29)

    def rows(z, carry):
        out[pl.ds(RATES * z, 3), :] = feed[z, pl.ds(start, 3), :]
        out[pl.ds(RATES * z + 3, 3), :] = decay[z, pl.ds(start, 3), :]
        return carry

    lax.fori_loop(0, NZ, rows, 0, unroll=8)
    out[pl.ds(RATES * NZ, 8), :] = jnp.zeros((8, NX), jnp.float32)


def pack_rates(feed, decay):
    return pallas(pack_rates_kernel, "pack_rates", 4, out_shape=vmem(RATE_ROWS, NX))(feed, decay)


def pack_y_kernel(which, u, v, feed, decay, x_b, x_a, _, out):
    even_x = is_even("gx")
    to_low = is_even("gy") if which else jnp.logical_not(is_even("gy"))
    inner = lanes()[1]
    top = lax.broadcasted_iota(jnp.int32, (8, NX), 0) < 4
    start, rate_start = jnp.where(to_low, OWN, OWN + 28), jnp.where(to_low, OWN, OWN + 29)

    def rows(z, carry):
        out[pl.ds(FIELDS * z, 4), :] = u[z, pl.ds(start, 4), :]
        out[pl.ds(FIELDS * z + 4, 4), :] = v[z, pl.ds(start, 4), :]
        if not which:
            out[pl.ds(TAIL + RATES * z, 3), :] = feed[z, pl.ds(rate_start, 3), :]
            out[pl.ds(TAIL + RATES * z + 3, 3), :] = decay[z, pl.ds(rate_start, 3), :]
        return carry

    lax.fori_loop(0, NZ, rows, 0, unroll=8)
    if not which:
        out[pl.ds(TAIL + RATES * NZ, 8), :] = jnp.zeros((8, NX), jnp.float32)

    def corner(j, carry):
        made = []
        for first, base in ((0, 0), (4, 12)):
            sides = []
            for is_right in (True, False):
                value = None
                for n in range(4):
                    b, a = x_b[n, j], x_a[n, j]
                    halo = jnp.where(even_x, a, b) if is_right else jnp.where(even_x, b, a)
                    here = (inner >= 4 * n) & (inner < 4 * n + 4)
                    halo = turn(halo, 4 * n - base)
                    value = halo if n == 0 else jnp.where(here, halo, value)
                sides.append(turn(value, (0 if is_right else 4) - first, 0))
            made.append(jnp.where(top, sides[0], sides[1]))
        out[pl.ds(CORNER + 8 * j, 8), :] = jnp.where(to_low, made[0], made[1])
        return carry

    lax.fori_loop(0, GZ, corner, 0, unroll=True)


def pack_y(which, u, v, feed, decay, x_b, x_a, after):
    return pallas(
        functools.partial(pack_y_kernel, which),
        "pack_odd" if which else "pack_even",
        8,
        out_shape=vmem(TAIL + (0 if which else RATE_ROWS), NX),
        in_specs=[pl.BlockSpec(memory_space=pltpu.VMEM)] * 6 + [pl.BlockSpec(memory_space=pl.ANY)],
    )(u, v, feed, decay, x_b, x_a, after)


def x_sums(src_u, src_v, z, rows):
    sums = []
    for ref in (src_u, src_v):
        for row in rows:
            value = ref[z, pl.ds(row, 8), :]
            sums.append(turn(value, 1) + turn(value, -1))
    return tuple(sums)


def step_rows(src_u, src_v, feed, decay, z, below, above, row, x_u, x_v):
    at, down, up = pl.ds(row, 8), pl.ds(row - 1, 8), pl.ds(row + 1, 8)
    u, v, f = src_u[z, at, :], src_v[z, at, :], feed[z, at, :]
    near_u = x_u + (src_u[z, down, :] + src_u[z, up, :])
    near_v = x_v + (src_v[z, down, :] + src_v[z, up, :])
    along_u = src_u[below, at, :] + src_u[above, at, :]
    along_v = src_v[below, at, :] + src_v[above, at, :]
    react = u * (v * v)
    new_u = (0.24 * near_u + 0.01 * along_u) + (f - u * (f - 0.02)) - react
    new_v = (0.12 * near_v + 0.005 * along_v) + decay[z, at, :] * v + react
    return new_u, new_v


def sweep(src, rates, rows, count, place, emit, unroll):
    def body(i, sums):
        z, below, above = place(i)
        ahead = x_sums(*src, place(jnp.minimum(i + 1, count - 1))[0], rows)
        values = [
            step_rows(*src, *rates, z, below, above, row, sums[n], sums[len(rows) + n])
            for n, row in enumerate(rows)
        ]
        emit(z, values)
        return ahead

    lax.fori_loop(0, count, body, x_sums(*src, place(0)[0], rows), unroll=unroll)


def to_planes(dst, rows):
    def emit(z, values):
        for row, new in zip(rows, values):
            for ref, value in zip(dst, new):
                ref[z, pl.ds(row, 8), :] = value

    return emit


def main_place(i):
    return i, jnp.maximum(i - 1, 0), jnp.minimum(i + 1, NZ - 1)


def strip_place(i):
    z = jnp.where(i < GZ, i + RIGHT, i - GZ + LEFT)
    return z, z - 1, z + 1


def strip_ends(refs, rows, group):
    for ref in refs:
        for plane in (RIGHT, LEFT):
            for row in rows:
                at = pl.ds(row, 8)
                first, last = ref[plane, at, :], ref[plane + GZ - 1, at, :]
                ref[plane - 1, at, :] = jnp.where(group == 0, first, turn(last, 16))
                ref[plane + GZ, at, :] = jnp.where(group == GROUPS - 1, last, turn(first, -16))


def merge_strips(src, dst, rows, inner):
    for old, new in zip(src, dst):
        for j in range(GZ):
            for row in rows:
                at = pl.ds(row, 8)
                new[j, at, :] = jnp.where(inner < 8, old[j + RIGHT, at, :], old[j + LEFT, at, :])


def with_edges(merged, z, row, value, edge):
    g = lax.div(z, GZ)
    piece = merged[z - g * GZ, pl.ds(row, 8), :]
    return jnp.where(edge, pltpu.roll(piece, NX - 8 - 16 * g, 1), value)


INNER_ROWS = (8, 16, 24, 32)
LAST_INNER_ROWS = (12, 20, 28)


EARLY_STEPS = 2


def early_kernel(
    u0, v0, feed, decay, x_b, x_a, su0_in, sv0_in, s_feed_in, s_decay_in,
    su0, sv0, s_feed, s_decay, su1, sv1, su2, sv2, su3, sv3, mu, mv, *fields_and_scratch,
):
    *fields, su4, sv4 = fields_and_scratch
    even_x = is_even("gx")
    lane, inner, group = lanes()
    right_halo = (inner >= 8) & (inner < 12)
    left_halo = (inner >= 4) & (inner < 8)

    def halos(j, carry):
        for n, ref in enumerate((su0, sv0, s_feed, s_decay)):
            b, a = x_b[n, j], x_a[n, j]
            on_right, on_left = jnp.where(even_x, a, b), jnp.where(even_x, b, a)
            for t in range(4):
                at = pl.ds(OWN + 8 * t, 8)
                both = ref[j + RIGHT, at, :]
                ref[j + RIGHT, at, :] = jnp.where(right_halo, turn(on_right, 8 - 4 * t), both)
                ref[j + LEFT, at, :] = jnp.where(left_halo, turn(on_left, 4 - 4 * t), both)
        return carry

    lax.fori_loop(0, GZ, halos, 0, unroll=True)

    levels = [(su0, sv0), (su1, sv1), (su2, sv2), (su3, sv3), (su4, sv4)]
    for step in range(STEPS):
        rows = INNER_ROWS if step < STEPS - 1 else LAST_INNER_ROWS
        strip_ends(levels[step], INNER_ROWS, group)
        emit = to_planes(levels[step + 1], rows)
        sweep(levels[step], (s_feed, s_decay), rows, 2 * GZ, strip_place, emit, 14)
    merge_strips((su4, sv4), (mu, mv), LAST_INNER_ROWS, inner)

    levels = [(u0, v0)] + list(zip(fields[::2], fields[1::2]))
    for step in range(EARLY_STEPS):
        emit = to_planes(levels[step + 1], INNER_ROWS)
        sweep(levels[step], (feed, decay), INNER_ROWS, NZ, main_place, emit, 14)


def early(u0, v0, feed, decay, x_b, x_a, su0, sv0, s_feed, s_decay):
    out = (vmem(*STRIP),) * 10 + (vmem(GZ, PY, NX),) * 2 + (vmem(*FIELD),) * (2 * EARLY_STEPS)
    return pallas(
        early_kernel,
        "early",
        4,
        20_000_000_000,
        out_shape=out,
        input_output_aliases={6: 0, 7: 1, 8: 2, 9: 3},
        scratch_shapes=[vmem(*STRIP)] * 2,
    )(u0, v0, feed, decay, x_b, x_a, su0, sv0, s_feed, s_decay)


def late_kernel(feed, decay, mu, mv, first_u, first_v, *outs):
    lane = lanes()[0]
    *fields, o_u, o_v = outs
    levels = [(first_u, first_v)] + list(zip(fields[::2], fields[1::2]))
    for step in range(STEPS - 1 - EARLY_STEPS):
        emit = to_planes(levels[step + 1], INNER_ROWS)
        sweep(levels[step], (feed, decay), INNER_ROWS, NZ, main_place, emit, 14)
    edge = (lane < 4) | (lane >= 124)

    def finish(z, values):
        for row, new in zip(LAST_INNER_ROWS, values):
            for out, merged, value in zip((o_u, o_v), (mu, mv), new):
                out[z, pl.ds(row - OWN, 8), :] = with_edges(merged, z, row, value, edge)

    sweep(levels[-1], (feed, decay), LAST_INNER_ROWS, NZ, main_place, finish, 14)


def late(feed, decay, mu, mv, first_u, first_v):
    out = (vmem(*FIELD),) * (2 * (STEPS - 1 - EARLY_STEPS)) + (vmem(NZ, NY, NX),) * 2
    return pallas(late_kernel, "late", 4, 20_000_000_000, out_shape=out)(feed, decay, mu, mv, first_u, first_v)


N_STATE = 22


def border_kernel(is_last, *refs):
    n_messages = 2 if is_last else 1
    messages = refs[:n_messages]
    state = refs[n_messages + N_STATE : n_messages + 2 * N_STATE]
    rest = refs[n_messages + 2 * N_STATE :]
    (u0, v0, feed, decay, su0, sv0, s_feed, s_decay) = state[:8]
    (su1, sv1, su2, sv2, su3, sv3, u1, v1, u2, v2, u3, v3, o_u, o_v) = state[8:]
    if is_last:
        (y, rate_src), tail = messages, 0
        out_u, out_v, su4, sv4, mu, mv, sems = rest
    else:
        y, rate_src, tail = messages[0], messages[0], TAIL
        su4, sv4, mu, mv = rest
    is_low = is_even("gy") if is_last else jnp.logical_not(is_even("gy"))
    lane, inner, group = lanes()
    to, rate_to = jnp.where(is_low, LOW, HIGH), jnp.where(is_low, LOW + 1, HIGH)
    tile, last_tile, out_row = jnp.where(is_low, 4, 36), jnp.where(is_low, 8, 36), jnp.where(is_low, 0, NY - 4)

    def rows(z, carry):
        u0[z, pl.ds(to, 4), :] = y[pl.ds(FIELDS * z, 4), :]
        v0[z, pl.ds(to, 4), :] = y[pl.ds(FIELDS * z + 4, 4), :]
        feed[z, pl.ds(rate_to, 3), :] = rate_src[pl.ds(tail + RATES * z, 3), :]
        decay[z, pl.ds(rate_to, 3), :] = rate_src[pl.ds(tail + RATES * z + 3, 3), :]
        return carry

    lax.fori_loop(0, NZ, rows, 0, unroll=8)

    right_halo = (inner >= 8) & (inner < 12)
    left_halo = (inner >= 4) & (inner < 8)

    def strip(j, carry):
        fields = rates = None
        for g in range(GROUPS):
            z = GZ * g + j
            one = turn(y[pl.ds(FIELDS * z, 8), :], 16 * g + 8)
            two = turn(rate_src[pl.ds(tail + RATES * z, 8), :], 16 * g + 8)
            fields = one if g == 0 else jnp.where(group == g, one, fields)
            rates = two if g == 0 else jnp.where(group == g, two, rates)
        corner = y[pl.ds(CORNER + 8 * j, 8), :]
        other = turn(corner, 4, 0)
        for plane, mask, lane_at, top, bottom in (
            (j + RIGHT, right_halo, 8, corner, other),
            (j + LEFT, left_halo, 4, other, corner),
        ):
            su0[plane, pl.ds(to, 4), :] = jnp.where(mask, turn(top, lane_at), fields)[:4]
            sv0[plane, pl.ds(to, 4), :] = jnp.where(mask, turn(bottom, lane_at - 4), fields)[4:]
            s_feed[plane, pl.ds(rate_to, 3), :] = rates[:3]
            s_decay[plane, pl.ds(rate_to, 3), :] = rates[3:6]
            for n, ref in ((2, s_feed), (3, s_decay)):
                halo = turn(top, lane_at - 4 * n)[:4]
                at = pl.ds(to, 4)
                ref[plane, at, :] = jnp.where(mask[:4], halo, ref[plane, at, :])
        return carry

    lax.fori_loop(0, GZ, strip, 0, unroll=True)

    levels = [(su0, sv0), (su1, sv1), (su2, sv2), (su3, sv3), (su4, sv4)]
    for step in range(STEPS):
        now = (tile,) if step < STEPS - 1 else (last_tile,)
        strip_ends(levels[step], (tile,), group)
        sweep(levels[step], (s_feed, s_decay), now, 2 * GZ, strip_place, to_planes(levels[step + 1], now), 14)
    merge_strips((su4, sv4), (mu, mv), (last_tile,), inner)

    levels = [(u0, v0), (u1, v1), (u2, v2), (u3, v3)]
    for step in range(STEPS - 1):
        sweep(levels[step], (feed, decay), (tile,), NZ, main_place, to_planes(levels[step + 1], (tile,)), 28)
    edge = (lane < 4) | (lane >= 124)

    def finish(z, values):
        for out, merged, value in zip((o_u, o_v), (mu, mv), values[0]):
            out[z, pl.ds(out_row, 4), :] = with_edges(merged, z, last_tile, value, edge)[:4]

    if not is_last:
        sweep(levels[-1], (feed, decay), (last_tile,), NZ, main_place, finish, 28)
        return
    copies = []
    parts = 2
    part = NZ // parts
    for c in range(parts):

        def place(i, c=c):
            return main_place(i + c * part)

        sweep(levels[-1], (feed, decay), (last_tile,), part, place, finish, part)
        for n, (src, dst) in enumerate(((o_u, out_u), (o_v, out_v))):
            at = pl.ds(c * part, part)
            copies.append(pltpu.make_async_copy(src.at[at], dst.at[at], sems.at[2 * c + n]))
            copies[-1].start()
    for copy in copies:
        copy.wait()


def border(messages, state):
    is_last = len(messages) == 2
    out = tuple(vmem(*a.shape) for a in state)
    specs = [pl.BlockSpec(memory_space=pltpu.VMEM)] * N_STATE
    scratch = [vmem(*STRIP)] * 2 + [vmem(GZ, PY, NX)] * 2
    if is_last:
        out += (jax.ShapeDtypeStruct((NZ, NY, NX), jnp.float32),) * 2
        specs += [pl.BlockSpec(memory_space=pltpu.HBM)] * 2
        scratch += [pltpu.SemaphoreType.DMA((4,))]
    return pallas(
        functools.partial(border_kernel, is_last),
        "border_odd" if is_last else "border_even",
        4,
        20_000_000_000,
        out_shape=out,
        out_specs=tuple(specs),
        input_output_aliases={len(messages) + n: n for n in range(N_STATE)},
        scratch_shapes=scratch,
    )(*messages, *state)


def shards(activator, inhibitor, feed_rate, kill_rate):
    u0, v0, feed, decay, su0, sv0, s_feed, s_decay, x_send_b, x_send_a = load(
        activator, inhibitor, feed_rate, kill_rate
    )
    x_b = swap(x_send_b, "gx", 1)
    x_a = swap(x_send_a, "gx", 0)
    rates, x_b, x_a = lax.optimization_barrier((pack_rates(feed, decay), x_b, x_a))
    half_way = relay(rates, "gy")
    send_b = pack_y(1, u0, v0, feed, decay, x_b, x_a, rates)
    y_b = swap(send_b, "gy", 1)
    send_a = pack_y(0, u0, v0, feed, decay, x_b, x_a, send_b)
    y_a = swap(send_a, "gy", 0)
    x_b, _ = lax.optimization_barrier((x_b, send_a))
    made = early(u0, v0, feed, decay, x_b, x_a, su0, sv0, s_feed, s_decay)
    strips, (mu, mv), fields = made[:10], made[10:12], made[12:]
    half_way, mu = lax.optimization_barrier((half_way, mu))
    r_b = after_relay(half_way, "gy")
    rest = late(feed, decay, mu, mv, *fields[-2:])
    state = border((y_a,), (u0, v0, feed, decay, *strips, *fields, *rest))
    return border((y_b, r_b), state)[N_STATE:]


def solution(mesh):
    spec = P(None, "gy", "gx")
    return jax.shard_map(
        shards, mesh=mesh, in_specs=(spec,) * 4, out_specs=(spec,) * 2, check_vma=False
    )
```

```python
import functools

import jax
import jax.numpy as jnp
from jax import lax
from jax.experimental import pallas as pl
from jax.experimental.pallas import tpu as pltpu
from jax.sharding import PartitionSpec as P

STEPS = 4
NZ, NY, NX = 56, 32, 128
W = 4
PY = 48
OWN, LOW, HIGH = 8, 4, 40
GROUPS, GZ = 8, NZ // 8
FIELDS, RATES = 2 * W, 2 * (W - 1)
CORNER = NZ * FIELDS
TAIL = CORNER + 8 * GZ
MESSAGE = (TAIL + NZ * RATES + 8, NX)
RIGHT, LEFT = 1, GZ + 3
SPLANES = 2 * GZ + 4


def swap_pairs(count, parity):
    pairs = []
    for low in range(parity, count, 2):
        high = (low + 1) % count
        pairs += [(low, high), (high, low)]
    return pairs


def swap(block, axis, parity):
    return lax.ppermute(block, axis, swap_pairs(lax.axis_size(axis), parity))


def is_even(axis):
    return lax.rem(lax.axis_index(axis), 2) == 0


def lanes():
    lane = lax.broadcasted_iota(jnp.int32, (8, NX), 1)
    return lane, lax.rem(lane, 16), lax.div(lane, 16)


def turn(value, shift, axis=1):
    shift = shift % value.shape[axis]
    return value if shift == 0 else pltpu.roll(value, shift, axis)


def vmem(*shape):
    return pltpu.VMEM(shape, jnp.float32)


FIELD = (NZ, PY, NX)
STRIP = (SPLANES, PY, NX)
EDGE = (4, GZ, 8, NX)


def pallas(kernel, name, megabytes, flops=0, **kwargs):
    return pl.pallas_call(
        kernel,
        name=name,
        compiler_params=pltpu.CompilerParams(vmem_limit_bytes=megabytes * 1024 * 1024),
        cost_estimate=pl.CostEstimate(flops=flops, bytes_accessed=flops // 4, transcendentals=0),
        **kwargs,
    )


def load_kernel(u, v, f, k, pu, pv, feed, decay, su, sv, s_feed, s_decay, out_b, out_a, fs, ks, sems):
    own = pl.ds(OWN, NY)
    copies = [
        pltpu.make_async_copy(f, fs, sems.at[0]),
        pltpu.make_async_copy(k, ks, sems.at[1]),
        pltpu.make_async_copy(u, pu.at[:, own, :], sems.at[2]),
        pltpu.make_async_copy(v, pv.at[:, own, :], sems.at[3]),
    ]
    for copy in copies:
        copy.start()
    even = is_even("gx")
    _, inner, group = lanes()

    def rates(z, carry):
        for t in range(0, 4, 2):
            at, to = pl.ds(pl.multiple_of(z * NY, NY) + 8 * t, 16), pl.ds(OWN + 8 * t, 16)
            rate = fs[at, :].astype(jnp.float32)
            feed[z, to, :] = rate
            decay[z, to, :] = 0.51 - (rate + ks[at, :].astype(jnp.float32))
        return carry

    copies[0].wait()
    copies[1].wait()
    lax.fori_loop(0, NZ, rates, 0, unroll=14)

    def pack(arrays):
        def body(j, carry):
            for n, src, dst in arrays:
                left_edge = right_edge = None
                for t in range(4):
                    at = pl.ds(OWN + 8 * t, 8)
                    both = None
                    for g in range(GROUPS):
                        value = turn(src[GZ * g + j, at, :], 16 * g + 8)
                        both = value if g == 0 else jnp.where(group == g, value, both)
                    dst[j + RIGHT, at, :] = both
                    dst[j + LEFT, at, :] = both
                    low, high = turn(both, 4 * t - 8), turn(both, 4 * t - 4)
                    here = (inner >= 4 * t) & (inner < 4 * t + 4)
                    left_edge = low if t == 0 else jnp.where(here, low, left_edge)
                    right_edge = high if t == 0 else jnp.where(here, high, right_edge)
                out_b[n, j] = jnp.where(even, left_edge, right_edge)
                out_a[n, j] = jnp.where(even, right_edge, left_edge)
            return carry

        lax.fori_loop(0, GZ, body, 0, unroll=2)

    pack(((2, feed, s_feed), (3, decay, s_decay)))
    copies[2].wait()
    copies[3].wait()
    pack(((0, pu, su), (1, pv, sv)))


def load(u, v, f, k):
    f, k = f.reshape(NZ * NY, NX), k.reshape(NZ * NY, NX)
    u, v, f, k = (pltpu.with_memory_space_constraint(a, pltpu.HBM) for a in (u, v, f, k))
    rates = pltpu.VMEM((NZ * NY, NX), jnp.bfloat16)
    return pallas(
        load_kernel,
        "load",
        8,
        out_shape=(vmem(*FIELD),) * 4 + (vmem(*STRIP),) * 4 + (vmem(*EDGE),) * 2,
        in_specs=[pl.BlockSpec(memory_space=pltpu.HBM)] * 4,
        scratch_shapes=[rates, rates, pltpu.SemaphoreType.DMA((4,))],
    )(u, v, f, k)


def pack_y_kernel(which, u, v, feed, decay, x_b, x_a, _, out):
    even_x = is_even("gx")
    to_low = is_even("gy") if which else jnp.logical_not(is_even("gy"))
    inner = lanes()[1]
    top = lax.broadcasted_iota(jnp.int32, (8, NX), 0) < 4
    start, rate_start = jnp.where(to_low, OWN, OWN + 28), jnp.where(to_low, OWN, OWN + 29)

    def rows(z, carry):
        out[pl.ds(FIELDS * z, 4), :] = u[z, pl.ds(start, 4), :]
        out[pl.ds(FIELDS * z + 4, 4), :] = v[z, pl.ds(start, 4), :]
        out[pl.ds(TAIL + RATES * z, 3), :] = feed[z, pl.ds(rate_start, 3), :]
        out[pl.ds(TAIL + RATES * z + 3, 3), :] = decay[z, pl.ds(rate_start, 3), :]
        return carry

    lax.fori_loop(0, NZ, rows, 0, unroll=8)
    out[pl.ds(TAIL + RATES * NZ, 8), :] = jnp.zeros((8, NX), jnp.float32)

    def corner(j, carry):
        made = []
        for first, base in ((0, 0), (4, 12)):
            sides = []
            for is_right in (True, False):
                value = None
                for n in range(4):
                    b, a = x_b[n, j], x_a[n, j]
                    halo = jnp.where(even_x, a, b) if is_right else jnp.where(even_x, b, a)
                    here = (inner >= 4 * n) & (inner < 4 * n + 4)
                    halo = turn(halo, 4 * n - base)
                    value = halo if n == 0 else jnp.where(here, halo, value)
                sides.append(turn(value, (0 if is_right else 4) - first, 0))
            made.append(jnp.where(top, sides[0], sides[1]))
        out[pl.ds(CORNER + 8 * j, 8), :] = jnp.where(to_low, made[0], made[1])
        return carry

    lax.fori_loop(0, GZ, corner, 0, unroll=True)


def pack_y(which, u, v, feed, decay, x_b, x_a, after):
    return pallas(
        functools.partial(pack_y_kernel, which),
        "pack_odd" if which else "pack_even",
        8,
        out_shape=vmem(*MESSAGE),
        in_specs=[pl.BlockSpec(memory_space=pltpu.VMEM)] * 6 + [pl.BlockSpec(memory_space=pl.ANY)],
    )(u, v, feed, decay, x_b, x_a, after)


def x_sums(src_u, src_v, z, rows):
    sums = []
    for ref in (src_u, src_v):
        for row in rows:
            value = ref[z, pl.ds(row, 8), :]
            sums.append(turn(value, 1) + turn(value, -1))
    return tuple(sums)


def step_rows(src_u, src_v, feed, decay, z, below, above, row, x_u, x_v):
    at, down, up = pl.ds(row, 8), pl.ds(row - 1, 8), pl.ds(row + 1, 8)
    u, v, f = src_u[z, at, :], src_v[z, at, :], feed[z, at, :]
    near_u = x_u + (src_u[z, down, :] + src_u[z, up, :])
    near_v = x_v + (src_v[z, down, :] + src_v[z, up, :])
    along_u = src_u[below, at, :] + src_u[above, at, :]
    along_v = src_v[below, at, :] + src_v[above, at, :]
    react = u * (v * v)
    new_u = (0.24 * near_u + 0.01 * along_u) + (f - u * (f - 0.02)) - react
    new_v = (0.12 * near_v + 0.005 * along_v) + decay[z, at, :] * v + react
    return new_u, new_v


def sweep(src, rates, rows, count, place, emit, unroll):
    def body(i, sums):
        z, below, above = place(i)
        ahead = x_sums(*src, place(jnp.minimum(i + 1, count - 1))[0], rows)
        values = [
            step_rows(*src, *rates, z, below, above, row, sums[n], sums[len(rows) + n])
            for n, row in enumerate(rows)
        ]
        emit(z, values)
        return ahead

    lax.fori_loop(0, count, body, x_sums(*src, place(0)[0], rows), unroll=unroll)


def to_planes(dst, rows):
    def emit(z, values):
        for row, new in zip(rows, values):
            for ref, value in zip(dst, new):
                ref[z, pl.ds(row, 8), :] = value

    return emit


def main_place(i):
    return i, jnp.maximum(i - 1, 0), jnp.minimum(i + 1, NZ - 1)


def strip_place(i):
    z = jnp.where(i < GZ, i + RIGHT, i - GZ + LEFT)
    return z, z - 1, z + 1


def strip_ends(refs, rows, group):
    for ref in refs:
        for plane in (RIGHT, LEFT):
            for row in rows:
                at = pl.ds(row, 8)
                first, last = ref[plane, at, :], ref[plane + GZ - 1, at, :]
                ref[plane - 1, at, :] = jnp.where(group == 0, first, turn(last, 16))
                ref[plane + GZ, at, :] = jnp.where(group == GROUPS - 1, last, turn(first, -16))


def merge_strips(src, dst, rows, inner):
    for old, new in zip(src, dst):
        for j in range(GZ):
            for row in rows:
                at = pl.ds(row, 8)
                new[j, at, :] = jnp.where(inner < 8, old[j + RIGHT, at, :], old[j + LEFT, at, :])


def with_edges(merged, z, row, value, edge):
    g = lax.div(z, GZ)
    piece = merged[z - g * GZ, pl.ds(row, 8), :]
    return jnp.where(edge, pltpu.roll(piece, NX - 8 - 16 * g, 1), value)


INNER_ROWS = (8, 16, 24, 32)
LAST_INNER_ROWS = (12, 20, 28)


EARLY_STEPS = 2


def early_kernel(
    u0, v0, feed, decay, x_b, x_a, su0_in, sv0_in, s_feed_in, s_decay_in,
    su0, sv0, s_feed, s_decay, su1, sv1, su2, sv2, su3, sv3, mu, mv, *fields_and_scratch,
):
    *fields, su4, sv4 = fields_and_scratch
    even_x = is_even("gx")
    lane, inner, group = lanes()
    right_halo = (inner >= 8) & (inner < 12)
    left_halo = (inner >= 4) & (inner < 8)

    def halos(j, carry):
        for n, ref in enumerate((su0, sv0, s_feed, s_decay)):
            b, a = x_b[n, j], x_a[n, j]
            on_right, on_left = jnp.where(even_x, a, b), jnp.where(even_x, b, a)
            for t in range(4):
                at = pl.ds(OWN + 8 * t, 8)
                both = ref[j + RIGHT, at, :]
                ref[j + RIGHT, at, :] = jnp.where(right_halo, turn(on_right, 8 - 4 * t), both)
                ref[j + LEFT, at, :] = jnp.where(left_halo, turn(on_left, 4 - 4 * t), both)
        return carry

    lax.fori_loop(0, GZ, halos, 0, unroll=True)

    levels = [(su0, sv0), (su1, sv1), (su2, sv2), (su3, sv3), (su4, sv4)]
    for step in range(STEPS):
        rows = INNER_ROWS if step < STEPS - 1 else LAST_INNER_ROWS
        strip_ends(levels[step], INNER_ROWS, group)
        emit = to_planes(levels[step + 1], rows)
        sweep(levels[step], (s_feed, s_decay), rows, 2 * GZ, strip_place, emit, 14)
    merge_strips((su4, sv4), (mu, mv), LAST_INNER_ROWS, inner)

    levels = [(u0, v0)] + list(zip(fields[::2], fields[1::2]))
    for step in range(EARLY_STEPS):
        emit = to_planes(levels[step + 1], INNER_ROWS)
        sweep(levels[step], (feed, decay), INNER_ROWS, NZ, main_place, emit, 28)


def early(u0, v0, feed, decay, x_b, x_a, su0, sv0, s_feed, s_decay):
    out = (vmem(*STRIP),) * 10 + (vmem(GZ, PY, NX),) * 2 + (vmem(*FIELD),) * (2 * EARLY_STEPS)
    return pallas(
        early_kernel,
        "early",
        4,
        20_000_000_000,
        out_shape=out,
        input_output_aliases={6: 0, 7: 1, 8: 2, 9: 3},
        scratch_shapes=[vmem(*STRIP)] * 2,
    )(u0, v0, feed, decay, x_b, x_a, su0, sv0, s_feed, s_decay)


def late_kernel(feed, decay, mu, mv, first_u, first_v, *outs):
    lane = lanes()[0]
    *fields, o_u, o_v = outs
    levels = [(first_u, first_v)] + list(zip(fields[::2], fields[1::2]))
    for step in range(STEPS - 1 - EARLY_STEPS):
        emit = to_planes(levels[step + 1], INNER_ROWS)
        sweep(levels[step], (feed, decay), INNER_ROWS, NZ, main_place, emit, 28)
    edge = (lane < 4) | (lane >= 124)

    def finish(z, values):
        for row, new in zip(LAST_INNER_ROWS, values):
            for out, merged, value in zip((o_u, o_v), (mu, mv), new):
                out[z, pl.ds(row - OWN, 8), :] = with_edges(merged, z, row, value, edge)

    sweep(levels[-1], (feed, decay), LAST_INNER_ROWS, NZ, main_place, finish, 28)


def late(feed, decay, mu, mv, first_u, first_v):
    out = (vmem(*FIELD),) * (2 * (STEPS - 1 - EARLY_STEPS)) + (vmem(NZ, NY, NX),) * 2
    return pallas(late_kernel, "late", 4, 20_000_000_000, out_shape=out)(feed, decay, mu, mv, first_u, first_v)


N_STATE = 22


def border_kernel(is_last, *refs):
    y, state, rest = refs[0], refs[1 + N_STATE : 1 + 2 * N_STATE], refs[1 + 2 * N_STATE :]
    (u0, v0, feed, decay, su0, sv0, s_feed, s_decay) = state[:8]
    (su1, sv1, su2, sv2, su3, sv3, u1, v1, u2, v2, u3, v3, o_u, o_v) = state[8:]
    if is_last:
        out_u, out_v, su4, sv4, mu, mv, sems = rest
    else:
        su4, sv4, mu, mv = rest
    is_low = is_even("gy") if is_last else jnp.logical_not(is_even("gy"))
    lane, inner, group = lanes()
    to, rate_to = jnp.where(is_low, LOW, HIGH), jnp.where(is_low, LOW + 1, HIGH)
    tile, last_tile, out_row = jnp.where(is_low, 4, 36), jnp.where(is_low, 8, 36), jnp.where(is_low, 0, NY - 4)

    def rows(z, carry):
        u0[z, pl.ds(to, 4), :] = y[pl.ds(FIELDS * z, 4), :]
        v0[z, pl.ds(to, 4), :] = y[pl.ds(FIELDS * z + 4, 4), :]
        feed[z, pl.ds(rate_to, 3), :] = y[pl.ds(TAIL + RATES * z, 3), :]
        decay[z, pl.ds(rate_to, 3), :] = y[pl.ds(TAIL + RATES * z + 3, 3), :]
        return carry

    lax.fori_loop(0, NZ, rows, 0, unroll=8)

    right_halo = (inner >= 8) & (inner < 12)
    left_halo = (inner >= 4) & (inner < 8)

    def strip(j, carry):
        fields = rates = None
        for g in range(GROUPS):
            z = GZ * g + j
            one = turn(y[pl.ds(FIELDS * z, 8), :], 16 * g + 8)
            two = turn(y[pl.ds(TAIL + RATES * z, 8), :], 16 * g + 8)
            fields = one if g == 0 else jnp.where(group == g, one, fields)
            rates = two if g == 0 else jnp.where(group == g, two, rates)
        corner = y[pl.ds(CORNER + 8 * j, 8), :]
        other = turn(corner, 4, 0)
        for plane, mask, lane_at, top, bottom in (
            (j + RIGHT, right_halo, 8, corner, other),
            (j + LEFT, left_halo, 4, other, corner),
        ):
            su0[plane, pl.ds(to, 4), :] = jnp.where(mask, turn(top, lane_at), fields)[:4]
            sv0[plane, pl.ds(to, 4), :] = jnp.where(mask, turn(bottom, lane_at - 4), fields)[4:]
            s_feed[plane, pl.ds(rate_to, 3), :] = rates[:3]
            s_decay[plane, pl.ds(rate_to, 3), :] = rates[3:6]
            for n, ref in ((2, s_feed), (3, s_decay)):
                halo = turn(top, lane_at - 4 * n)[:4]
                at = pl.ds(to, 4)
                ref[plane, at, :] = jnp.where(mask[:4], halo, ref[plane, at, :])
        return carry

    lax.fori_loop(0, GZ, strip, 0, unroll=True)

    levels = [(su0, sv0), (su1, sv1), (su2, sv2), (su3, sv3), (su4, sv4)]
    for step in range(STEPS):
        now = (tile,) if step < STEPS - 1 else (last_tile,)
        strip_ends(levels[step], (tile,), group)
        sweep(levels[step], (s_feed, s_decay), now, 2 * GZ, strip_place, to_planes(levels[step + 1], now), 14)
    merge_strips((su4, sv4), (mu, mv), (last_tile,), inner)

    levels = [(u0, v0), (u1, v1), (u2, v2), (u3, v3)]
    for step in range(STEPS - 1):
        sweep(levels[step], (feed, decay), (tile,), NZ, main_place, to_planes(levels[step + 1], (tile,)), 56)
    edge = (lane < 4) | (lane >= 124)

    def finish(z, values):
        for out, merged, value in zip((o_u, o_v), (mu, mv), values[0]):
            out[z, pl.ds(out_row, 4), :] = with_edges(merged, z, last_tile, value, edge)[:4]

    if not is_last:
        sweep(levels[-1], (feed, decay), (last_tile,), NZ, main_place, finish, 56)
        return
    copies = []
    parts = 2
    part = NZ // parts
    for c in range(parts):

        def place(i, c=c):
            return main_place(i + c * part)

        sweep(levels[-1], (feed, decay), (last_tile,), part, place, finish, part)
        for n, (src, dst) in enumerate(((o_u, out_u), (o_v, out_v))):
            at = pl.ds(c * part, part)
            copies.append(pltpu.make_async_copy(src.at[at], dst.at[at], sems.at[2 * c + n]))
            copies[-1].start()
    for copy in copies:
        copy.wait()


def border(is_last, message, state):
    out = tuple(vmem(*a.shape) for a in state)
    specs = [pl.BlockSpec(memory_space=pltpu.VMEM)] * N_STATE
    scratch = [vmem(*STRIP)] * 2 + [vmem(GZ, PY, NX)] * 2
    if is_last:
        out += (jax.ShapeDtypeStruct((NZ, NY, NX), jnp.float32),) * 2
        specs += [pl.BlockSpec(memory_space=pltpu.HBM)] * 2
        scratch += [pltpu.SemaphoreType.DMA((4,))]
    return pallas(
        functools.partial(border_kernel, is_last),
        "border_odd" if is_last else "border_even",
        4,
        20_000_000_000,
        out_shape=out,
        out_specs=tuple(specs),
        input_output_aliases={1 + n: n for n in range(N_STATE)},
        scratch_shapes=scratch,
    )(message, *state)


def shards(activator, inhibitor, feed_rate, kill_rate):
    u0, v0, feed, decay, su0, sv0, s_feed, s_decay, x_send_b, x_send_a = load(
        activator, inhibitor, feed_rate, kill_rate
    )
    x_b = swap(x_send_b, "gx", 1)
    x_a = swap(x_send_a, "gx", 0)
    send_b = pack_y(1, u0, v0, feed, decay, x_b, x_a, feed)
    y_b = swap(send_b, "gy", 1)
    send_a = pack_y(0, u0, v0, feed, decay, x_b, x_a, send_b)
    y_a = swap(send_a, "gy", 0)
    x_b, _ = lax.optimization_barrier((x_b, send_a))
    made = early(u0, v0, feed, decay, x_b, x_a, su0, sv0, s_feed, s_decay)
    strips, (mu, mv), fields = made[:10], made[10:12], made[12:]
    rest = late(feed, decay, mu, mv, *fields[-2:])
    state = border(False, y_a, (u0, v0, feed, decay, *strips, *fields, *rest))
    return border(True, y_b, state)[N_STATE:]


def solution(mesh):
    spec = P(None, "gy", "gx")
    return jax.shard_map(
        shards, mesh=mesh, in_specs=(spec,) * 4, out_specs=(spec,) * 2, check_vma=False
    )
```

```python
import functools

import jax
import jax.numpy as jnp
from jax import lax
from jax.experimental import pallas as pl
from jax.experimental.pallas import tpu as pltpu
from jax.sharding import PartitionSpec as P

STEPS = 4
NZ, NY, NX = 56, 32, 128
W = 4
PY = 48
OWN, LOW, HIGH = 8, 4, 40
GROUPS, GZ = 8, NZ // 8
FIELDS, RATES = 2 * W, 2 * (W - 1)
TAIL = NZ * FIELDS
CORNER = TAIL + NZ * RATES
MESSAGE = (CORNER + 8 * GZ, NX)
RIGHT, LEFT = 1, GZ + 3
SPLANES = 2 * GZ + 4


def swap_pairs(count, parity):
    pairs = []
    for low in range(parity, count, 2):
        high = (low + 1) % count
        pairs += [(low, high), (high, low)]
    return pairs


def swap(block, axis, parity):
    return lax.ppermute(block, axis, swap_pairs(lax.axis_size(axis), parity))


def is_even(axis):
    return lax.rem(lax.axis_index(axis), 2) == 0


def lanes():
    lane = lax.broadcasted_iota(jnp.int32, (8, NX), 1)
    return lane, lax.rem(lane, 16), lax.div(lane, 16)


def turn(value, shift, axis=1):
    shift = shift % value.shape[axis]
    return value if shift == 0 else pltpu.roll(value, shift, axis)


def vmem(*shape):
    return pltpu.VMEM(shape, jnp.float32)


FIELD = (NZ, PY, NX)
STRIP = (SPLANES, PY, NX)
EDGE = (4, GZ, 8, NX)


def pallas(kernel, name, megabytes, flops=0, **kwargs):
    return pl.pallas_call(
        kernel,
        name=name,
        compiler_params=pltpu.CompilerParams(vmem_limit_bytes=megabytes * 1024 * 1024),
        cost_estimate=pl.CostEstimate(flops=flops, bytes_accessed=flops // 4, transcendentals=0),
        **kwargs,
    )


def load_kernel(u, v, f, k, pu, pv, feed, decay, su, sv, s_feed, s_decay, out_b, out_a, fs, ks, sems):
    own = pl.ds(OWN, NY)
    copies = [
        pltpu.make_async_copy(f, fs, sems.at[0]),
        pltpu.make_async_copy(k, ks, sems.at[1]),
        pltpu.make_async_copy(u, pu.at[:, own, :], sems.at[2]),
        pltpu.make_async_copy(v, pv.at[:, own, :], sems.at[3]),
    ]
    for copy in copies:
        copy.start()
    even = is_even("gx")
    _, inner, group = lanes()

    def rates(z, carry):
        for t in range(0, 4, 2):
            at, to = pl.ds(pl.multiple_of(z * NY, NY) + 8 * t, 16), pl.ds(OWN + 8 * t, 16)
            rate = fs[at, :].astype(jnp.float32)
            feed[z, to, :] = rate
            decay[z, to, :] = 0.51 - (rate + ks[at, :].astype(jnp.float32))
        return carry

    copies[0].wait()
    copies[1].wait()
    lax.fori_loop(0, NZ, rates, 0, unroll=14)

    def strips_of(arrays, j):
        made = []
        for _, src, dst in arrays:
            for t in range(4):
                at = pl.ds(OWN + 8 * t, 8)
                both = None
                for g in range(GROUPS):
                    value = turn(src[GZ * g + j, at, :], 16 * g + 8)
                    both = value if g == 0 else jnp.where(group == g, value, both)
                dst[j + RIGHT, at, :] = both
                dst[j + LEFT, at, :] = both
                made.append(both)
        return tuple(made)

    def edges_of(arrays, j, strips):
        for a, (n, _, _) in enumerate(arrays):
            left_edge = right_edge = None
            for t in range(4):
                both = strips[4 * a + t]
                low, high = turn(both, 4 * t - 8), turn(both, 4 * t - 4)
                here = (inner >= 4 * t) & (inner < 4 * t + 4)
                left_edge = low if t == 0 else jnp.where(here, low, left_edge)
                right_edge = high if t == 0 else jnp.where(here, high, right_edge)
            out_b[n, j] = jnp.where(even, left_edge, right_edge)
            out_a[n, j] = jnp.where(even, right_edge, left_edge)

    def pack(arrays):
        def body(j, strips):
            made = strips_of(arrays, j)
            edges_of(arrays, j - 1, strips)
            return made

        last = lax.fori_loop(1, GZ, body, strips_of(arrays, 0), unroll=3)
        edges_of(arrays, GZ - 1, last)

    pack(((2, feed, s_feed), (3, decay, s_decay)))
    copies[2].wait()
    copies[3].wait()
    pack(((0, pu, su), (1, pv, sv)))


def load(u, v, f, k):
    f, k = f.reshape(NZ * NY, NX), k.reshape(NZ * NY, NX)
    u, v, f, k = (pltpu.with_memory_space_constraint(a, pltpu.HBM) for a in (u, v, f, k))
    rates = pltpu.VMEM((NZ * NY, NX), jnp.bfloat16)
    return pallas(
        load_kernel,
        "load",
        8,
        out_shape=(vmem(*FIELD),) * 4 + (vmem(*STRIP),) * 4 + (vmem(*EDGE),) * 2,
        in_specs=[pl.BlockSpec(memory_space=pltpu.HBM)] * 4,
        scratch_shapes=[rates, rates, pltpu.SemaphoreType.DMA((4,))],
    )(u, v, f, k)


def pack_y_kernel(which, u, v, feed, decay, x_b, x_a, _, out):
    even_x = is_even("gx")
    to_low = is_even("gy") if which else jnp.logical_not(is_even("gy"))
    inner = lanes()[1]
    top = lax.broadcasted_iota(jnp.int32, (8, NX), 0) < 4
    start, rate_start = jnp.where(to_low, OWN, OWN + 28), jnp.where(to_low, OWN, OWN + 29)

    def rows(z, carry):
        out[pl.ds(FIELDS * z, 4), :] = u[z, pl.ds(start, 4), :]
        out[pl.ds(FIELDS * z + 4, 4), :] = v[z, pl.ds(start, 4), :]
        out[pl.ds(TAIL + RATES * z, 3), :] = feed[z, pl.ds(rate_start, 3), :]
        out[pl.ds(TAIL + RATES * z + 3, 3), :] = decay[z, pl.ds(rate_start, 3), :]
        return carry

    lax.fori_loop(0, NZ, rows, 0, unroll=8)

    def corner(j, carry):
        made = []
        for first, base in ((0, 0), (4, 12)):
            sides = []
            for is_right in (True, False):
                value = None
                for n in range(4):
                    b, a = x_b[n, j], x_a[n, j]
                    halo = jnp.where(even_x, a, b) if is_right else jnp.where(even_x, b, a)
                    here = (inner >= 4 * n) & (inner < 4 * n + 4)
                    halo = turn(halo, 4 * n - base)
                    value = halo if n == 0 else jnp.where(here, halo, value)
                sides.append(turn(value, (0 if is_right else 4) - first, 0))
            made.append(jnp.where(top, sides[0], sides[1]))
        out[pl.ds(CORNER + 8 * j, 8), :] = jnp.where(to_low, made[0], made[1])
        return carry

    lax.fori_loop(0, GZ, corner, 0, unroll=True)


def pack_y(which, u, v, feed, decay, x_b, x_a, after):
    return pallas(
        functools.partial(pack_y_kernel, which),
        "pack_odd" if which else "pack_even",
        8,
        out_shape=vmem(*MESSAGE),
        in_specs=[pl.BlockSpec(memory_space=pltpu.VMEM)] * 6 + [pl.BlockSpec(memory_space=pl.ANY)],
    )(u, v, feed, decay, x_b, x_a, after)


def x_sums(src_u, src_v, z, rows):
    sums = []
    for ref in (src_u, src_v):
        for row in rows:
            value = ref[z, pl.ds(row, 8), :]
            sums.append(turn(value, 1) + turn(value, -1))
    return tuple(sums)


def step_rows(src_u, src_v, feed, decay, z, below, above, row, x_u, x_v):
    at, down, up = pl.ds(row, 8), pl.ds(row - 1, 8), pl.ds(row + 1, 8)
    u, v, f = src_u[z, at, :], src_v[z, at, :], feed[z, at, :]
    near_u = x_u + (src_u[z, down, :] + src_u[z, up, :])
    near_v = x_v + (src_v[z, down, :] + src_v[z, up, :])
    along_u = src_u[below, at, :] + src_u[above, at, :]
    along_v = src_v[below, at, :] + src_v[above, at, :]
    react = u * (v * v)
    new_u = (0.24 * near_u + 0.01 * along_u) + (f - u * (f - 0.02)) - react
    new_v = (0.12 * near_v + 0.005 * along_v) + decay[z, at, :] * v + react
    return new_u, new_v


def sweep(src, rates, rows, count, place, emit, unroll):
    def body(i, sums):
        z, below, above = place(i)
        ahead = x_sums(*src, place(jnp.minimum(i + 1, count - 1))[0], rows)
        values = [
            step_rows(*src, *rates, z, below, above, row, sums[n], sums[len(rows) + n])
            for n, row in enumerate(rows)
        ]
        emit(z, values)
        return ahead

    lax.fori_loop(0, count, body, x_sums(*src, place(0)[0], rows), unroll=unroll)


def to_planes(dst, rows):
    def emit(z, values):
        for row, new in zip(rows, values):
            for ref, value in zip(dst, new):
                ref[z, pl.ds(row, 8), :] = value

    return emit


def main_place(i):
    return i, jnp.maximum(i - 1, 0), jnp.minimum(i + 1, NZ - 1)


def strip_place(i):
    z = jnp.where(i < GZ, i + RIGHT, i - GZ + LEFT)
    return z, z - 1, z + 1


def strip_ends(refs, rows, group):
    for ref in refs:
        for plane in (RIGHT, LEFT):
            for row in rows:
                at = pl.ds(row, 8)
                first, last = ref[plane, at, :], ref[plane + GZ - 1, at, :]
                ref[plane - 1, at, :] = jnp.where(group == 0, first, turn(last, 16))
                ref[plane + GZ, at, :] = jnp.where(group == GROUPS - 1, last, turn(first, -16))


def merge_strips(src, dst, rows, inner):
    for old, new in zip(src, dst):
        for j in range(GZ):
            for row in rows:
                at = pl.ds(row, 8)
                new[j, at, :] = jnp.where(inner < 8, old[j + RIGHT, at, :], old[j + LEFT, at, :])


def with_edges(merged, z, row, value, edge):
    g = lax.div(z, GZ)
    piece = merged[z - g * GZ, pl.ds(row, 8), :]
    return jnp.where(edge, pltpu.roll(piece, NX - 8 - 16 * g, 1), value)


INNER_ROWS = (8, 16, 24, 32)
LAST_INNER_ROWS = (12, 20, 28)


EARLY_STEPS = 2


def early_kernel(
    u0, v0, feed, decay, x_b, x_a, su0_in, sv0_in, s_feed_in, s_decay_in,
    su0, sv0, s_feed, s_decay, su1, sv1, su2, sv2, su3, sv3, mu, mv, *fields_and_scratch,
):
    *fields, su4, sv4 = fields_and_scratch
    even_x = is_even("gx")
    lane, inner, group = lanes()
    right_halo = (inner >= 8) & (inner < 12)
    left_halo = (inner >= 4) & (inner < 8)

    def halos(j, carry):
        for n, ref in enumerate((su0, sv0, s_feed, s_decay)):
            b, a = x_b[n, j], x_a[n, j]
            on_right, on_left = jnp.where(even_x, a, b), jnp.where(even_x, b, a)
            for t in range(4):
                at = pl.ds(OWN + 8 * t, 8)
                both = ref[j + RIGHT, at, :]
                ref[j + RIGHT, at, :] = jnp.where(right_halo, turn(on_right, 8 - 4 * t), both)
                ref[j + LEFT, at, :] = jnp.where(left_halo, turn(on_left, 4 - 4 * t), both)
        return carry

    lax.fori_loop(0, GZ, halos, 0, unroll=True)

    levels = [(su0, sv0), (su1, sv1), (su2, sv2), (su3, sv3), (su4, sv4)]
    for step in range(STEPS):
        rows = INNER_ROWS if step < STEPS - 1 else LAST_INNER_ROWS
        strip_ends(levels[step], INNER_ROWS, group)
        emit = to_planes(levels[step + 1], rows)
        sweep(levels[step], (s_feed, s_decay), rows, 2 * GZ, strip_place, emit, 14)
    merge_strips((su4, sv4), (mu, mv), LAST_INNER_ROWS, inner)

    levels = [(u0, v0)] + list(zip(fields[::2], fields[1::2]))
    for step in range(EARLY_STEPS):
        emit = to_planes(levels[step + 1], INNER_ROWS)
        sweep(levels[step], (feed, decay), INNER_ROWS, NZ, main_place, emit, 28)


def early(u0, v0, feed, decay, x_b, x_a, su0, sv0, s_feed, s_decay):
    out = (vmem(*STRIP),) * 10 + (vmem(GZ, PY, NX),) * 2 + (vmem(*FIELD),) * (2 * EARLY_STEPS)
    return pallas(
        early_kernel,
        "early",
        4,
        20_000_000_000,
        out_shape=out,
        input_output_aliases={6: 0, 7: 1, 8: 2, 9: 3},
        scratch_shapes=[vmem(*STRIP)] * 2,
    )(u0, v0, feed, decay, x_b, x_a, su0, sv0, s_feed, s_decay)


def late_kernel(feed, decay, mu, mv, first_u, first_v, *outs):
    lane = lanes()[0]
    *fields, o_u, o_v = outs
    levels = [(first_u, first_v)] + list(zip(fields[::2], fields[1::2]))
    for step in range(STEPS - 1 - EARLY_STEPS):
        emit = to_planes(levels[step + 1], INNER_ROWS)
        sweep(levels[step], (feed, decay), INNER_ROWS, NZ, main_place, emit, 28)
    edge = (lane < 4) | (lane >= 124)

    def finish(z, values):
        for row, new in zip(LAST_INNER_ROWS, values):
            for out, merged, value in zip((o_u, o_v), (mu, mv), new):
                out[z, pl.ds(row - OWN, 8), :] = with_edges(merged, z, row, value, edge)

    sweep(levels[-1], (feed, decay), LAST_INNER_ROWS, NZ, main_place, finish, 28)


def late(feed, decay, mu, mv, first_u, first_v):
    out = (vmem(*FIELD),) * (2 * (STEPS - 1 - EARLY_STEPS)) + (vmem(NZ, NY, NX),) * 2
    return pallas(late_kernel, "late", 4, 20_000_000_000, out_shape=out)(feed, decay, mu, mv, first_u, first_v)


N_STATE = 22


def border_kernel(is_last, *refs):
    y, state, rest = refs[0], refs[1 + N_STATE : 1 + 2 * N_STATE], refs[1 + 2 * N_STATE :]
    (u0, v0, feed, decay, su0, sv0, s_feed, s_decay) = state[:8]
    (su1, sv1, su2, sv2, su3, sv3, u1, v1, u2, v2, u3, v3, o_u, o_v) = state[8:]
    if is_last:
        out_u, out_v, su4, sv4, mu, mv, sems = rest
    else:
        su4, sv4, mu, mv = rest
    is_low = is_even("gy") if is_last else jnp.logical_not(is_even("gy"))
    lane, inner, group = lanes()
    to, rate_to = jnp.where(is_low, LOW, HIGH), jnp.where(is_low, LOW + 1, HIGH)
    tile, last_tile, out_row = jnp.where(is_low, 4, 36), jnp.where(is_low, 8, 36), jnp.where(is_low, 0, NY - 4)

    def rows(z, carry):
        u0[z, pl.ds(to, 4), :] = y[pl.ds(FIELDS * z, 4), :]
        v0[z, pl.ds(to, 4), :] = y[pl.ds(FIELDS * z + 4, 4), :]
        feed[z, pl.ds(rate_to, 3), :] = y[pl.ds(TAIL + RATES * z, 3), :]
        decay[z, pl.ds(rate_to, 3), :] = y[pl.ds(TAIL + RATES * z + 3, 3), :]
        return carry

    lax.fori_loop(0, NZ, rows, 0, unroll=8)

    right_halo = (inner >= 8) & (inner < 12)
    left_halo = (inner >= 4) & (inner < 8)

    def strip(j, carry):
        fields = rates = None
        for g in range(GROUPS):
            z = GZ * g + j
            one = turn(y[pl.ds(FIELDS * z, 8), :], 16 * g + 8)
            two = turn(y[pl.ds(TAIL + RATES * z, 8), :], 16 * g + 8)
            fields = one if g == 0 else jnp.where(group == g, one, fields)
            rates = two if g == 0 else jnp.where(group == g, two, rates)
        corner = y[pl.ds(CORNER + 8 * j, 8), :]
        other = turn(corner, 4, 0)
        for plane, mask, lane_at, top, bottom in (
            (j + RIGHT, right_halo, 8, corner, other),
            (j + LEFT, left_halo, 4, other, corner),
        ):
            su0[plane, pl.ds(to, 4), :] = jnp.where(mask, turn(top, lane_at), fields)[:4]
            sv0[plane, pl.ds(to, 4), :] = jnp.where(mask, turn(bottom, lane_at - 4), fields)[4:]
            s_feed[plane, pl.ds(rate_to, 3), :] = rates[:3]
            s_decay[plane, pl.ds(rate_to, 3), :] = rates[3:6]
            for n, ref in ((2, s_feed), (3, s_decay)):
                halo = turn(top, lane_at - 4 * n)[:4]
                at = pl.ds(to, 4)
                ref[plane, at, :] = jnp.where(mask[:4], halo, ref[plane, at, :])
        return carry

    lax.fori_loop(0, GZ, strip, 0, unroll=True)

    levels = [(su0, sv0), (su1, sv1), (su2, sv2), (su3, sv3), (su4, sv4)]
    for step in range(STEPS):
        now = (tile,) if step < STEPS - 1 else (last_tile,)
        strip_ends(levels[step], (tile,), group)
        sweep(levels[step], (s_feed, s_decay), now, 2 * GZ, strip_place, to_planes(levels[step + 1], now), 14)
    merge_strips((su4, sv4), (mu, mv), (last_tile,), inner)

    levels = [(u0, v0), (u1, v1), (u2, v2), (u3, v3)]
    for step in range(STEPS - 1):
        sweep(levels[step], (feed, decay), (tile,), NZ, main_place, to_planes(levels[step + 1], (tile,)), 56)
    edge = (lane < 4) | (lane >= 124)

    def finish(z, values):
        for out, merged, value in zip((o_u, o_v), (mu, mv), values[0]):
            out[z, pl.ds(out_row, 4), :] = with_edges(merged, z, last_tile, value, edge)[:4]

    if not is_last:
        sweep(levels[-1], (feed, decay), (last_tile,), NZ, main_place, finish, 56)
        return
    copies = []
    parts = 2
    part = NZ // parts
    for c in range(parts):

        def place(i, c=c):
            return main_place(i + c * part)

        sweep(levels[-1], (feed, decay), (last_tile,), part, place, finish, part)
        for n, (src, dst) in enumerate(((o_u, out_u), (o_v, out_v))):
            at = pl.ds(c * part, part)
            copies.append(pltpu.make_async_copy(src.at[at], dst.at[at], sems.at[2 * c + n]))
            copies[-1].start()
    for copy in copies:
        copy.wait()


def border(is_last, message, state):
    out = tuple(vmem(*a.shape) for a in state)
    specs = [pl.BlockSpec(memory_space=pltpu.VMEM)] * N_STATE
    scratch = [vmem(*STRIP)] * 2 + [vmem(GZ, PY, NX)] * 2
    if is_last:
        out += (jax.ShapeDtypeStruct((NZ, NY, NX), jnp.float32),) * 2
        specs += [pl.BlockSpec(memory_space=pltpu.HBM)] * 2
        scratch += [pltpu.SemaphoreType.DMA((4,))]
    return pallas(
        functools.partial(border_kernel, is_last),
        "border_odd" if is_last else "border_even",
        4,
        20_000_000_000,
        out_shape=out,
        out_specs=tuple(specs),
        input_output_aliases={1 + n: n for n in range(N_STATE)},
        scratch_shapes=scratch,
    )(message, *state)


def shards(activator, inhibitor, feed_rate, kill_rate):
    u0, v0, feed, decay, su0, sv0, s_feed, s_decay, x_send_b, x_send_a = load(
        activator, inhibitor, feed_rate, kill_rate
    )
    x_b = swap(x_send_b, "gx", 1)
    x_a = swap(x_send_a, "gx", 0)
    send_b = pack_y(1, u0, v0, feed, decay, x_b, x_a, feed)
    y_b = swap(send_b, "gy", 1)
    send_a = pack_y(0, u0, v0, feed, decay, x_b, x_a, send_b)
    y_a = swap(send_a, "gy", 0)
    x_b, _ = lax.optimization_barrier((x_b, send_a))
    made = early(u0, v0, feed, decay, x_b, x_a, su0, sv0, s_feed, s_decay)
    strips, (mu, mv), fields = made[:10], made[10:12], made[12:]
    rest = late(feed, decay, mu, mv, *fields[-2:])
    state = border(False, y_a, (u0, v0, feed, decay, *strips, *fields, *rest))
    return border(True, y_b, state)[N_STATE:]


def solution(mesh):
    spec = P(None, "gy", "gx")
    return jax.shard_map(
        shards, mesh=mesh, in_specs=(spec,) * 4, out_specs=(spec,) * 2, check_vma=False
    )
```
